32 devices in a mesh: group: 2 (over y), lat: 4 (over z), lon: 2 (over x), fld: 2 (over core).
Axes of the slice: x: 2, y: 2, z: 4, core: 2. Of those that a mesh axis runs over, the one named last changes fastest.
Arguments:
- exchange_density_arrays: bfloat16 [24, 336, 1440], P(('group', 'fld'), 'lat', 'lon'), parts along dimension 0, may hold values from -6 to 6
- marine_thermal_frozen_values: float32 [4, 1008, 4320], P(('group', 'fld'), 'lat', 'lon'), parts along dimension 0, may hold values from -6 to 6
- coarse_continent_flag: int32 [336, 1440], P('lat', 'lon'), may hold values 0 or 1
- marine_continent_flag: int32 [1008, 4320], P('lat', 'lon'), may hold values 0 or 1
- parallel_source_initial: int32 [1008], replicated, may hold values from 0 to 332, as said below
- parallel_source_tally: int32 [1008], replicated, may hold values from 1 to 4
- parallel_intersect_coefs: bfloat16 [1008, 4], replicated, may hold values from 0.25 to 1
- meridian_source_displacement: int32 [4320], replicated, may hold values from 0 to 4
- meridian_source_tally: int32 [4320], replicated, may hold values from 1 to 5
- meridian_intersect_coefs: bfloat16 [4320, 5], replicated, may hold values from 0.25 to 1
Outputs:
- ocean_flux: bfloat16 [24, 1008, 4320], P(('group', 'fld'), 'lat', 'lon'), parts along dimension 0
- coarse_boundary_values: float32 [4, 336, 1440], P(('group', 'fld'), 'lat', 'lon'), parts along dimension 0
The draws below stay inside these ranges and needn't reach their ends.
There are 2 independent parts, one for each index of `group`. The reference program is written for one: setup_inputs(seed, part) draws one part's arguments, and reference() takes and returns one part's arrays. A program takes and returns all parts, laid end to end along the dimension named above; an argument that names none is the same for every part. Nothing has to cross between parts.
Inputs may be any that keep to these rules, and one draw needn't show every extreme that they name: `parallel_source_initial`: nondecreasing along the ocean rows; the first entry is 0.
All inputs are finite; a program needn't handle non-finite values. No bound on the sum of `coarse_continent_flag` or of `marine_continent_flag` on one device may be relied on, other than what follows from the above.
Results may differ from the reference program's by a relative error of at most 0.001.
Values may be sent and summed in bfloat16 or wider, within the bound.
A program may use at most 192 MiB of HBM per device.

```python
import math
import jax
import jax.numpy as jnp
from jax import lax

NA = 336
MA = 1440
FIELDS = 12
FEEDBACK_VARS = 2
LAT_TAPS = 4
LON_REACH = 4
LON_TAPS = 5
MARINE_PARALLELS = 1008
MARINE_MERIDIANS = 4320


def draw_parallel_source_initial(key, part):
    key = jax.random.fold_in(key, 11)
    scoring_random_key, extra_random_key = jax.random.split(key)
    between = MARINE_PARALLELS - 1
    scores = jax.random.randint(scoring_random_key, (between,), 0, 1 << 16)
    region_labels = jax.random.randint(extra_random_key, (8,), 0, 2)
    region_of = jnp.arange(between, dtype=jnp.int32) * 8 // between
    scores = (scores + region_labels[region_of] * (1 << 17)) * 4096 + jnp.arange(between, dtype=jnp.int32)
    picked = lax.top_k(scores, NA - LAT_TAPS)[1]
    rising = jnp.zeros((between,), jnp.int32).at[picked].set(1)
    return jnp.concatenate([jnp.zeros((1,), jnp.int32), jnp.cumsum(rising).astype(jnp.int32)])


def set_ends(values, own_key, smallest, top_value):
    longest = values.shape.index(max(values.shape))
    spots = []
    for shift in (0, 1):
        where = [jax.random.randint(jax.random.fold_in(own_key, axis), (), 0, length) for axis, length in enumerate(values.shape)]
        where[longest] = (where[longest] + shift) % values.shape[longest]
        spots.append(tuple(where))
    return values.at[spots[0]].set(smallest).at[spots[1]].set(top_value)


def block_scale(stream_key, extent, pieces, smallest, high):
    factor_of = 1.0
    for position, blocks in pieces:
        heights = jax.random.uniform(jax.random.fold_in(jax.random.fold_in(stream_key, 6), position), (blocks,), jnp.float32, smallest / len(pieces), high / len(pieces))
        factor_of = factor_of * jnp.repeat(jnp.exp(heights), extent[position] // blocks).reshape((-1,) + (1,) * (len(extent) - 1 - position))
    return factor_of


def gaussian(rng, extent, deviation, bound, cuts=(), held_as=jnp.bfloat16):
    gain = block_scale(rng, extent, cuts, -0.22, 0.18) if cuts else 1.0
    array = jax.random.normal(rng, extent, jnp.float32) * deviation * gain
    return jnp.minimum(jnp.maximum(array, -bound), bound).astype(held_as)


def setup_inputs(seed: int = 0, part: int = 0) -> dict:
    splits = jax.random.split(jax.random.key(seed), 11)
    part_splits = jax.random.split(jax.random.fold_in(splits[10], part), 11)
    return {
        "exchange_density_arrays": gaussian(part_splits[0], (FIELDS, NA, MA), 1.0, 6.0, ((0, 2), (1, 4), (2, 2))),
        "marine_thermal_frozen_values": gaussian(part_splits[1], (FEEDBACK_VARS, MARINE_PARALLELS, MARINE_MERIDIANS), 1.0, 6.0, ((0, 2), (1, 4), (2, 2)), jnp.float32),
        "coarse_continent_flag": set_ends((jax.random.randint(splits[2], (NA, MA), 0, 10) < 3).astype(jnp.int32), jax.random.fold_in(splits[2], 1), 0, 1),
        "marine_continent_flag": set_ends((jax.random.randint(splits[3], (MARINE_PARALLELS, MARINE_MERIDIANS), 0, 10) < 3).astype(jnp.int32), jax.random.fold_in(splits[3], 1), 0, 1),
        "parallel_source_initial": draw_parallel_source_initial(jax.random.fold_in(splits[10], 71), part),
        "parallel_source_tally": set_ends(jax.random.randint(splits[5], (MARINE_PARALLELS,), 1, LAT_TAPS + 1), jax.random.fold_in(splits[5], 1), 1, LAT_TAPS).astype(jnp.int32),
        "parallel_intersect_coefs": jnp.clip(jnp.exp(jax.random.uniform(splits[6], (MARINE_PARALLELS, LAT_TAPS), jnp.float32, math.log(0.25), math.log(1.0))), 0.25, 1.0).astype(jnp.bfloat16),
        "meridian_source_displacement": set_ends(jax.random.randint(splits[7], (MARINE_MERIDIANS,), 0, LON_REACH + 1), jax.random.fold_in(splits[7], 1), 0, LON_REACH).astype(jnp.int32),
        "meridian_source_tally": set_ends(jax.random.randint(splits[8], (MARINE_MERIDIANS,), 1, LON_TAPS + 1), jax.random.fold_in(splits[8], 1), 1, LON_TAPS).astype(jnp.int32),
        "meridian_intersect_coefs": jnp.clip(jnp.exp(jax.random.uniform(splits[9], (MARINE_MERIDIANS, LON_TAPS), jnp.float32, math.log(0.25), math.log(1.0))), 0.25, 1.0).astype(jnp.bfloat16),
    }


FLOOR_SHARE = 0.25


def tap_weights(widths, weights):
    tap_count = weights.shape[1]
    allowed = jnp.arange(tap_count, dtype=jnp.int32)[None, :] < widths[:, None]
    return jnp.where(allowed, weights.astype(jnp.float32), jnp.float32(0.0))


def reference(exchange_density_arrays, marine_thermal_frozen_values, coarse_continent_flag, marine_continent_flag, parallel_source_initial, parallel_source_tally, parallel_intersect_coefs, meridian_source_displacement, meridian_source_tally, meridian_intersect_coefs):
    row_taps = tap_weights(parallel_source_tally, parallel_intersect_coefs)
    col_taps = tap_weights(meridian_source_tally, meridian_intersect_coefs)
    row_index = (parallel_source_initial[:, None] + jnp.arange(LAT_TAPS, dtype=jnp.int32)[None, :]).astype(jnp.int32)
    col_first = jnp.arange(MARINE_MERIDIANS, dtype=jnp.int32) // 3 - LON_REACH + meridian_source_displacement
    col_index = ((col_first[:, None] + jnp.arange(LON_TAPS, dtype=jnp.int32)[None, :]) % MA).astype(jnp.int32)
    water_atmos = (1 - coarse_continent_flag).astype(jnp.float32)
    marine_liquid_portion = (1 - marine_continent_flag).astype(jnp.float32)

    def forward(channel):
        stretched = jnp.zeros((MARINE_PARALLELS, MA), jnp.float32)
        for tap_index in range(LAT_TAPS):
            stretched = stretched + row_taps[:, tap_index, None] * jnp.take(channel, row_index[:, tap_index], axis=0)
        result = jnp.zeros((MARINE_PARALLELS, MARINE_MERIDIANS), jnp.float32)
        for tap_index in range(LON_TAPS):
            result = result + col_taps[None, :, tap_index] * jnp.take(stretched, col_index[:, tap_index], axis=1)
        return result

    def backward(channel):
        narrowed = jnp.zeros((MARINE_PARALLELS, MA), jnp.float32)
        for tap_index in range(LON_TAPS):
            narrowed = narrowed.at[:, col_index[:, tap_index]].add(col_taps[None, :, tap_index] * channel)
        result = jnp.zeros((NA, MA), jnp.float32)
        for tap_index in range(LAT_TAPS):
            result = result.at[row_index[:, tap_index]].add(row_taps[:, tap_index, None] * narrowed)
        return result

    flux_denominator = forward(water_atmos)
    floor_flux = FLOOR_SHARE * jnp.sum(row_taps, axis=1)[:, None] * jnp.sum(col_taps, axis=1)[None, :]
    safe_flux = jnp.maximum(flux_denominator, floor_flux)

    def finish_flux(channel):
        numerator = forward(channel.astype(jnp.float32) * water_atmos)
        return (marine_liquid_portion * numerator / safe_flux).astype(jnp.bfloat16)

    ocean_flux = lax.map(finish_flux, exchange_density_arrays)

    surface_denominator = backward(marine_liquid_portion)
    lat_sums = jnp.zeros((NA,), jnp.float32).at[row_index.reshape(-1)].add(row_taps.reshape(-1))
    lon_sums = jnp.zeros((MA,), jnp.float32).at[col_index.reshape(-1)].add(col_taps.reshape(-1))
    floor_surface = FLOOR_SHARE * (lat_sums[:, None] * lon_sums[None, :] + 1.0)
    safe_surface = jnp.maximum(surface_denominator, floor_surface)

    def entire_boundary_values(channel):
        return backward(channel * marine_liquid_portion) / safe_surface

    coarse_boundary_values = lax.map(entire_boundary_values, marine_thermal_frozen_values)
    return ocean_flux, coarse_boundary_values
```

```python
import jax
import jax.numpy as jnp
import numpy as np
from jax import lax
from jax.experimental import pallas as pl
from jax.experimental.pallas import tpu as pltpu
from jax.sharding import PartitionSpec as P

LON_REACH = 4
FLOOR_SHARE = 0.25
TILE = 256
LANE = 128
VMEM_LIMIT = 56 * 1024 * 1024


def round_up(value, unit):
    return (value + unit - 1) // unit * unit


def neighbour(block, axis, step):
    count = lax.axis_size(axis)
    return lax.ppermute(block, axis, [(i, (i + step) % count) for i in range(count)])


def tap_weights(widths, weights):
    tap_count = weights.shape[1]
    allowed = jnp.arange(tap_count, dtype=jnp.int32)[None, :] < widths[:, None]
    return jnp.where(allowed, weights.astype(jnp.float32), jnp.float32(0.0))


def tile_chunks(atmos_cols, ocean_cols):
    tiles = -(-ocean_cols // TILE)
    chunk_total = round_up(atmos_cols + 2 * LON_REACH, LANE) // LANE
    table = []
    for tile in range(tiles):
        first = tile * TILE
        last = min(first + TILE, ocean_cols) - 1
        slots = range(first // 3 - LON_REACH, last // 3 + LON_REACH + 1)
        chunks = sorted({(s if s >= 0 else atmos_cols + 2 * LON_REACH + s) // LANE for s in slots})
        assert len(chunks) <= 2
        if len(chunks) == 1:
            chunks.append((chunks[0] + 1) % chunk_total)
        table.append(chunks)
    return np.array(table, np.int32), chunk_total


def column_tiles(shift, col_taps, chunk_table, atmos_cols):
    tiles = chunk_table.shape[0]
    cols = shift.shape[0]
    pad = tiles * TILE - cols
    taps = jnp.pad(col_taps, ((0, pad), (0, 0))).T.reshape(-1, tiles, 1, TILE)
    first = jnp.arange(cols, dtype=jnp.int32) // 3 - LON_REACH + shift
    first = jnp.pad(first, (0, pad)).reshape(tiles, 1, TILE)
    slots = chunk_table[:, :, None] * LANE + np.arange(LANE)[None, None, :]
    slots = slots.reshape(tiles, TILE, 1)
    wide = atmos_cols + 2 * LON_REACH
    offset = np.where(slots < atmos_cols + LON_REACH, slots, np.where(slots < wide, slots - wide, -100))
    offset = jnp.asarray(offset.astype(np.int32))
    result = jnp.zeros((tiles, TILE, TILE), jnp.float32)
    for k in range(col_taps.shape[1]):
        result = result + jnp.where(offset == first + k, taps[k], jnp.float32(0.0))
    return result.astype(jnp.bfloat16)


def row_matrix(first_row, row_taps, atmos_total):
    index = jnp.arange(atmos_total, dtype=jnp.int32)[None, :]
    result = jnp.zeros((first_row.shape[0], atmos_total), jnp.float32)
    for k in range(row_taps.shape[1]):
        result = result + jnp.where(index == (first_row + k)[:, None], row_taps[:, k][:, None], 0.0)
    return result


def split(value):
    high = value.astype(jnp.bfloat16)
    low = (value - high.astype(jnp.float32)).astype(jnp.bfloat16)
    return high, low


def forward_kernel(
    chunk_ref, x_ref, p_ref, q_ref, rows_ref, cols_ref, flag_ref, out_ref, high_ref, low_ref
):
    tile = pl.program_id(0)
    shards, channels = x_ref.shape[:2]
    chunk_total = high_ref.shape[0]
    ocean_rows = flag_ref.shape[0]

    @pl.when(tile == 0)
    def _():
        for ch in range(channels):
            value = None
            for s in range(shards):
                part = jnp.dot(p_ref[s], x_ref[s, ch], preferred_element_type=jnp.float32)
                value = part if value is None else value + part
            high, low = split(value)
            for c in range(chunk_total):
                high_ref[c, ch] = high[:, c * LANE : (c + 1) * LANE]
                low_ref[c, ch] = low[:, c * LANE : (c + 1) * LANE]

    first, second = chunk_ref[2 * tile], chunk_ref[2 * tile + 1]
    weights = q_ref[0]

    def spread(ch):
        high = jnp.concatenate([high_ref[first, ch], high_ref[second, ch]], axis=1)
        low = jnp.concatenate([low_ref[first, ch], low_ref[second, ch]], axis=1)
        value = jnp.dot(high, weights, preferred_element_type=jnp.float32)
        value = value + jnp.dot(low, weights, preferred_element_type=jnp.float32)
        return value[:ocean_rows]

    floor = FLOOR_SHARE * rows_ref[...] * cols_ref[...]
    water = (1 - flag_ref[...]).astype(jnp.float32)
    factor = water / jnp.maximum(spread(channels - 1), floor)
    for ch in range(channels - 1):
        out_ref[ch] = (spread(ch) * factor).astype(out_ref.dtype)


def forward_call(x, p, q, chunk_table, chunk_total, row_sums, col_sums, flag):
    shards, channels, atmos_rows, width = x.shape
    rows_padded = p.shape[1]
    ocean_rows, ocean_cols = flag.shape
    tiles = q.shape[0]
    whole = lambda *shape: pl.BlockSpec(shape, lambda j, *_: (0,) * len(shape))
    return pl.pallas_call(
        forward_kernel,
        out_shape=jax.ShapeDtypeStruct((channels - 1, ocean_rows, ocean_cols), jnp.bfloat16),
        grid_spec=pltpu.PrefetchScalarGridSpec(
            num_scalar_prefetch=1,
            grid=(tiles,),
            in_specs=[
                whole(*x.shape),
                whole(*p.shape),
                pl.BlockSpec((1, TILE, TILE), lambda j, *_: (j, 0, 0)),
                whole(ocean_rows, 1),
                pl.BlockSpec((1, TILE), lambda j, *_: (0, j)),
                pl.BlockSpec((ocean_rows, TILE), lambda j, *_: (0, j)),
            ],
            out_specs=pl.BlockSpec((channels - 1, ocean_rows, TILE), lambda j, *_: (0, 0, j)),
            scratch_shapes=[
                pltpu.VMEM((chunk_total, channels, rows_padded, LANE), jnp.bfloat16),
                pltpu.VMEM((chunk_total, channels, rows_padded, LANE), jnp.bfloat16),
            ],
        ),
        compiler_params=pltpu.CompilerParams(vmem_limit_bytes=VMEM_LIMIT),
        cost_estimate=pl.CostEstimate(
            flops=2 * channels * rows_padded * 2 * TILE * tiles * TILE,
            bytes_accessed=16 * 1024 * 1024,
            transcendentals=0,
        ),
        name="spread_fluxes",
    )(jnp.asarray(chunk_table.reshape(-1)), x, p, q, row_sums, col_sums, flag)


def backward_kernel(chunk_ref, field_ref, flag_ref, q_ref, pt_ref, out_ref, sum_ref):
    tile = pl.program_id(0)
    tiles = pl.num_programs(0)
    ocean_rows, ocean_cols = field_ref.shape[0], out_ref.shape[2]
    chunk_total = sum_ref.shape[0]

    @pl.when(tile == 0)
    def _():
        sum_ref[...] = jnp.zeros_like(sum_ref)

    limit = chunk_ref[chunk_ref.shape[0] - 1] - tile * TILE
    inside = lax.broadcasted_iota(jnp.int32, field_ref.shape, 1) < limit
    wet = inside & (flag_ref[...] == 0)
    high, low = split(jnp.where(wet, field_ref[...], 0.0))
    water = jnp.where(wet, 1.0, 0.0).astype(jnp.bfloat16)
    weights = q_ref[0]

    def fold(value):
        return lax.dot_general(
            value, weights, (((1,), (1,)), ((), ())), preferred_element_type=jnp.float32
        )

    first, second = chunk_ref[2 * tile], chunk_ref[2 * tile + 1]
    for ch, value in enumerate((fold(high) + fold(low), fold(water))):
        sum_ref[first, ch] += value[:, :LANE]
        sum_ref[second, ch] += value[:, LANE:]

    @pl.when(tile == tiles - 1)
    def _():
        matrix = pt_ref[...]
        for ch in range(2):
            for c in range(chunk_total):
                high, low = split(sum_ref[c, ch])
                total = jnp.dot(matrix, high, preferred_element_type=jnp.float32)
                total = total + jnp.dot(matrix, low, preferred_element_type=jnp.float32)
                out_ref[ch, :, c * LANE : (c + 1) * LANE] = total


def backward_call(field, flag, q, pt, chunk_table, chunk_total):
    ocean_rows, ocean_cols = flag.shape
    atmos_total = pt.shape[0]
    tiles = q.shape[0]
    table = np.concatenate([chunk_table.reshape(-1), [ocean_cols]]).astype(np.int32)
    return pl.pallas_call(
        backward_kernel,
        out_shape=jax.ShapeDtypeStruct((2, atmos_total, chunk_total * LANE), jnp.float32),
        grid_spec=pltpu.PrefetchScalarGridSpec(
            num_scalar_prefetch=1,
            grid=(tiles,),
            in_specs=[
                pl.BlockSpec((ocean_rows, TILE), lambda j, *_: (0, j)),
                pl.BlockSpec((ocean_rows, TILE), lambda j, *_: (0, j)),
                pl.BlockSpec((1, TILE, TILE), lambda j, *_: (j, 0, 0)),
                pl.BlockSpec(pt.shape, lambda j, *_: (0, 0)),
            ],
            out_specs=pl.BlockSpec(
                (2, atmos_total, chunk_total * LANE), lambda j, *_: (0, 0, 0)
            ),
            scratch_shapes=[pltpu.VMEM((chunk_total, 2, ocean_rows, LANE), jnp.float32)],
        ),
        compiler_params=pltpu.CompilerParams(vmem_limit_bytes=VMEM_LIMIT),
        cost_estimate=pl.CostEstimate(
            flops=2 * 3 * ocean_rows * TILE * tiles * TILE,
            bytes_accessed=8 * 1024 * 1024,
            transcendentals=0,
        ),
        name="fold_surface",
    )(jnp.asarray(table), field, flag, q, pt)


def longitude_sums(shift, col_taps, atmos_width, first_col, atmos_cols):
    total = jnp.zeros((atmos_width,), jnp.float32)
    shift = shift.reshape(atmos_width, 3)
    taps = col_taps.reshape(atmos_width, 3, -1)
    for offset in range(2 * LON_REACH + 1):
        part = jnp.zeros((atmos_width,), jnp.float32)
        for k in range(taps.shape[2]):
            part = part + jnp.sum(jnp.where(shift + k == offset, taps[:, :, k], 0.0), axis=1)
        total = total + jnp.roll(part, offset - LON_REACH)
    return lax.dynamic_slice_in_dim(total, first_col, atmos_cols)


def local(
    exchange_density_arrays,
    marine_thermal_frozen_values,
    coarse_continent_flag,
    marine_continent_flag,
    parallel_source_initial,
    parallel_source_tally,
    parallel_intersect_coefs,
    meridian_source_displacement,
    meridian_source_tally,
    meridian_intersect_coefs,
):
    band_pos = lax.axis_index("lat")
    tile_pos = lax.axis_index("lon")
    bands = lax.axis_size("lat")
    blocks = lax.axis_size("lon")
    atmos_rows, atmos_cols = coarse_continent_flag.shape
    ocean_rows, ocean_cols = marine_continent_flag.shape
    reach = LON_REACH
    atmos_total = atmos_rows * bands
    chunk_table, chunk_total = tile_chunks(atmos_cols, ocean_cols)
    width = chunk_total * LANE

    water_atmos = (1 - coarse_continent_flag).astype(jnp.bfloat16)
    stack = jnp.concatenate(
        [exchange_density_arrays * water_atmos[None], water_atmos[None]], axis=0
    )
    channels = stack.shape[0]
    right = neighbour(stack[:, :, :reach], "lon", -1)
    left = neighbour(stack[:, :, atmos_cols - reach :], "lon", 1)
    filler = jnp.zeros((channels, atmos_rows, width - atmos_cols - 2 * reach), jnp.bfloat16)
    stack = jnp.concatenate([stack, right, left, filler], axis=2)
    gathered = lax.all_gather(stack, "lat", axis=0, tiled=False)

    row_taps = tap_weights(parallel_source_tally, parallel_intersect_coefs)
    col_taps = tap_weights(meridian_source_tally, meridian_intersect_coefs)
    here = lambda array, pos, count: lax.dynamic_slice_in_dim(array, pos * count, count)
    my_rows = row_matrix(
        here(parallel_source_initial, band_pos, ocean_rows),
        here(row_taps, band_pos, ocean_rows),
        atmos_total,
    )
    my_cols = here(col_taps, tile_pos, ocean_cols)
    q = column_tiles(
        here(meridian_source_displacement, tile_pos, ocean_cols), my_cols, chunk_table, atmos_cols
    )
    row_sums = jnp.sum(my_rows, axis=1)[:, None]
    col_sums = jnp.sum(my_cols, axis=1)[None, :]

    partial = backward_call(
        marine_thermal_frozen_values[0],
        marine_continent_flag,
        q,
        my_rows.T.astype(jnp.bfloat16),
        chunk_table,
        chunk_total,
    )
    totals = lax.psum_scatter(partial, "lat", scatter_dimension=1, tiled=True)

    rows_padded = round_up(ocean_rows, 16)
    p = jnp.pad(my_rows.astype(jnp.bfloat16), ((0, rows_padded - ocean_rows), (0, 0)))
    p = p.reshape(rows_padded, bands, atmos_rows).transpose(1, 0, 2)
    ocean_flux = forward_call(
        gathered, p, q, chunk_table, chunk_total, row_sums, col_sums, marine_continent_flag
    )

    from_left = neighbour(totals[:, :, atmos_cols : atmos_cols + reach], "lon", 1)
    from_right = neighbour(totals[:, :, atmos_cols + reach : atmos_cols + 2 * reach], "lon", -1)
    rest = ((0, 0), (0, 0))
    totals = (
        totals[:, :, :atmos_cols]
        + jnp.pad(from_left, rest + ((0, atmos_cols - reach),))
        + jnp.pad(from_right, rest + ((atmos_cols - reach, 0),))
    )
    all_rows = row_matrix(parallel_source_initial - band_pos * atmos_rows, row_taps, atmos_rows)
    lat_sums = jnp.sum(all_rows, axis=0)
    lon_sums = longitude_sums(
        meridian_source_displacement,
        col_taps,
        atmos_cols * blocks,
        tile_pos * atmos_cols,
        atmos_cols,
    )
    safe_surface = jnp.maximum(
        totals[1], FLOOR_SHARE * (lat_sums[:, None] * lon_sums[None, :] + 1.0)
    )
    return ocean_flux, (totals[0] / safe_surface)[None]


def solution(mesh):
    fields = P(("group", "fld"), "lat", "lon")
    cells = P("lat", "lon")
    return jax.shard_map(
        local,
        mesh=mesh,
        in_specs=(fields, fields, cells, cells) + (P(),) * 6,
        out_specs=(fields, fields),
        check_vma=False,
    )
```

```python
import jax
import jax.numpy as jnp
import numpy as np
from jax import lax
from jax.experimental import pallas as pl
from jax.experimental.pallas import tpu as pltpu
from jax.sharding import PartitionSpec as P

LON_REACH = 4
FLOOR_SHARE = 0.25
TILE = 256
LANE = 128
VMEM_LIMIT = 56 * 1024 * 1024


def round_up(value, unit):
    return (value + unit - 1) // unit * unit


def neighbour(block, axis, step):
    count = lax.axis_size(axis)
    return lax.ppermute(block, axis, [(i, (i + step) % count) for i in range(count)])


def shift(block, axis, step):
    count = lax.axis_size(axis)
    pairs = [(i, i + step) for i in range(count) if 0 <= i + step < count]
    return lax.ppermute(block, axis, pairs)


def tap_weights(widths, weights):
    tap_count = weights.shape[1]
    allowed = jnp.arange(tap_count, dtype=jnp.int32)[None, :] < widths[:, None]
    return jnp.where(allowed, weights.astype(jnp.float32), jnp.float32(0.0))


def tile_chunks(atmos_cols, ocean_cols):
    tiles = -(-ocean_cols // TILE)
    chunk_total = round_up(atmos_cols + 2 * LON_REACH + 1, LANE) // LANE
    table = []
    for tile in range(tiles):
        first = tile * TILE
        last = min(first + TILE, ocean_cols) - 1
        slots = range(first // 3 - LON_REACH, last // 3 + LON_REACH + 1)
        chunks = sorted({(s if s >= 0 else atmos_cols + 2 * LON_REACH + s) // LANE for s in slots})
        assert len(chunks) <= 2
        if len(chunks) == 1:
            chunks.append((chunks[0] + 1) % chunk_total)
        table.append(chunks)
    return np.array(table, np.int32), chunk_total


def column_tiles(shift, col_taps, chunk_table, atmos_cols):
    tiles = chunk_table.shape[0]
    cols = shift.shape[0]
    pad = tiles * TILE - cols
    taps = jnp.pad(col_taps, ((0, pad), (0, 0))).T.reshape(-1, tiles, 1, TILE)
    first = jnp.arange(cols, dtype=jnp.int32) // 3 - LON_REACH + shift
    first = jnp.pad(first, (0, pad)).reshape(tiles, 1, TILE)
    slots = chunk_table[:, :, None] * LANE + np.arange(LANE)[None, None, :]
    slots = slots.reshape(tiles, TILE, 1)
    wide = atmos_cols + 2 * LON_REACH
    offset = np.where(slots < atmos_cols + LON_REACH, slots, np.where(slots < wide, slots - wide, -100))
    offset = jnp.asarray(offset.astype(np.int32))
    result = jnp.zeros((tiles, TILE, TILE), jnp.float32)
    for k in range(col_taps.shape[1]):
        result = result + jnp.where(offset == first + k, taps[k], jnp.float32(0.0))
    return result.astype(jnp.bfloat16)


def row_matrix(first_row, row_taps, atmos_total):
    index = jnp.arange(atmos_total, dtype=jnp.int32)[None, :]
    result = jnp.zeros((first_row.shape[0], atmos_total), jnp.float32)
    for k in range(row_taps.shape[1]):
        result = result + jnp.where(index == (first_row + k)[:, None], row_taps[:, k][:, None], 0.0)
    return result


def split(value):
    high = value.astype(jnp.bfloat16)
    low = (value - high.astype(jnp.float32)).astype(jnp.bfloat16)
    return high, low


def forward_kernel(blocks, chunk_ref, *refs):
    x_refs, p_refs = refs[:blocks], refs[blocks : 2 * blocks]
    q_ref, rows_ref, flag_ref, out_ref, high_ref, low_ref = refs[2 * blocks :]
    tile = pl.program_id(0)
    channels = x_refs[0].shape[0]
    chunk_total = high_ref.shape[0]
    ocean_rows = flag_ref.shape[1]

    @pl.when(tile == 0)
    def _():
        for ch in range(channels):
            value = None
            for x_ref, p_ref in zip(x_refs, p_refs):
                part = jnp.dot(p_ref[...], x_ref[ch], preferred_element_type=jnp.float32)
                value = part if value is None else value + part
            high, low = split(value.T)
            for c in range(chunk_total):
                high_ref[c, ch] = high[c * LANE : (c + 1) * LANE]
                low_ref[c, ch] = low[c * LANE : (c + 1) * LANE]

    first, second = chunk_ref[2 * tile], chunk_ref[2 * tile + 1]
    weights = q_ref[0].astype(jnp.float32).T
    col_sums = jnp.sum(weights, axis=1, keepdims=True)
    weights = weights.astype(jnp.bfloat16)

    def spread(ch):
        high = jnp.concatenate([high_ref[first, ch], high_ref[second, ch]], axis=0)
        low = jnp.concatenate([low_ref[first, ch], low_ref[second, ch]], axis=0)
        value = jnp.dot(weights, high, preferred_element_type=jnp.float32)
        value = value + jnp.dot(weights, low, preferred_element_type=jnp.float32)
        return value[:, :ocean_rows]

    floor = FLOOR_SHARE * rows_ref[...] * col_sums
    water = (1 - flag_ref[...]).astype(jnp.float32)
    factor = water / jnp.maximum(spread(channels - 1), floor)
    for ch in range(channels - 1):
        out_ref[ch] = (spread(ch) * factor).astype(out_ref.dtype)


def forward_call(pieces, matrices, q, chunk_table, chunk_total, row_sums, flag):
    blocks = len(pieces)
    channels = pieces[0].shape[0]
    rows_padded = matrices[0].shape[0]
    ocean_cols, ocean_rows = flag.shape
    tiles = q.shape[0]
    whole = lambda array: pl.BlockSpec(array.shape, lambda j, *_: (0,) * array.ndim)
    return pl.pallas_call(
        lambda *refs: forward_kernel(blocks, *refs),
        out_shape=jax.ShapeDtypeStruct((channels - 1, ocean_cols, ocean_rows), jnp.bfloat16),
        grid_spec=pltpu.PrefetchScalarGridSpec(
            num_scalar_prefetch=1,
            grid=(tiles,),
            in_specs=[whole(array) for array in (*pieces, *matrices)]
            + [
                pl.BlockSpec((1, TILE, TILE), lambda j, *_: (j, 0, 0)),
                whole(row_sums),
                pl.BlockSpec((TILE, ocean_rows), lambda j, *_: (j, 0)),
            ],
            out_specs=pl.BlockSpec((channels - 1, TILE, ocean_rows), lambda j, *_: (0, j, 0)),
            scratch_shapes=[
                pltpu.VMEM((chunk_total, channels, LANE, rows_padded), jnp.bfloat16),
                pltpu.VMEM((chunk_total, channels, LANE, rows_padded), jnp.bfloat16),
            ],
        ),
        compiler_params=pltpu.CompilerParams(vmem_limit_bytes=VMEM_LIMIT),
        cost_estimate=pl.CostEstimate(
            flops=2 * channels * rows_padded * 2 * TILE * tiles * TILE,
            bytes_accessed=16 * 1024 * 1024,
            transcendentals=0,
        ),
        name="spread_fluxes",
    )(jnp.asarray(chunk_table.reshape(-1)), *pieces, *matrices, q, row_sums, flag)


def backward_kernel(blocks, sizes, chunk_ref, field_ref, flag_ref, q_ref, *refs):
    ocean_rows, ocean_cols, wide = sizes
    matrix_refs, out_refs = refs[:blocks], refs[blocks : 2 * blocks]
    ones_ref, sum_ref = refs[2 * blocks :]
    tile = pl.program_id(0)
    chunk_total = sum_ref.shape[0]

    @pl.when(tile == 0)
    def _():
        lanes = lax.broadcasted_iota(jnp.int32, sum_ref.shape[1:], 2)
        for c in range(chunk_total):
            sum_ref[c] = jnp.where(lanes + c * LANE == wide, 1.0, 0.0)

    row = lax.broadcasted_iota(jnp.int32, field_ref.shape, 0)
    col = lax.broadcasted_iota(jnp.int32, field_ref.shape, 1)
    inside = col < ocean_cols - tile * TILE
    dry = flag_ref[...].astype(jnp.float32).T
    wet = inside & (row < ocean_rows) & (dry == 0.0)
    high, low = split(jnp.where(wet, field_ref[...], 0.0))
    water = jnp.where(wet | (inside & (row >= ocean_rows)), 1.0, 0.0).astype(jnp.bfloat16)
    weights = q_ref[0]

    def fold(value):
        return lax.dot_general(
            value, weights, (((1,), (1,)), ((), ())), preferred_element_type=jnp.float32
        )

    first, second = chunk_ref[2 * tile], chunk_ref[2 * tile + 1]
    for ch, value in enumerate((fold(high) + fold(low), fold(water))):
        sum_ref[first, ch] += value[:, :LANE]
        sum_ref[second, ch] += value[:, LANE:]

    @pl.when(tile == pl.num_programs(0) - 1)
    def _():
        for c in range(chunk_total):
            lanes = slice(c * LANE, (c + 1) * LANE)
            ones_ref[:, lanes] = sum_ref[c, 1, ocean_rows : ocean_rows + 1, :]
            for ch in range(2):
                high, low = split(sum_ref[c, ch])
                for matrix_ref, out_ref in zip(matrix_refs, out_refs):
                    matrix = matrix_ref[...]
                    total = jnp.dot(matrix, high, preferred_element_type=jnp.float32)
                    total = total + jnp.dot(matrix, low, preferred_element_type=jnp.float32)
                    out_ref[ch, :, lanes] = total


def backward_call(field, flag, q, matrices, chunk_table, chunk_total, wide):
    ocean_cols, ocean_rows = flag.shape
    rows_padded = matrices[0].shape[1]
    blocks = len(matrices)
    tiles = q.shape[0]
    width = chunk_total * LANE
    shapes = [(2, matrix.shape[0], width) for matrix in matrices] + [(1, width)]
    whole = lambda shape: pl.BlockSpec(shape, lambda j, *_: (0,) * len(shape))
    return pl.pallas_call(
        lambda *refs: backward_kernel(blocks, (ocean_rows, ocean_cols, wide), *refs),
        out_shape=[jax.ShapeDtypeStruct(shape, jnp.float32) for shape in shapes],
        grid_spec=pltpu.PrefetchScalarGridSpec(
            num_scalar_prefetch=1,
            grid=(tiles,),
            in_specs=[
                pl.BlockSpec((rows_padded, TILE), lambda j, *_: (0, j)),
                pl.BlockSpec((TILE, rows_padded), lambda j, *_: (j, 0)),
                pl.BlockSpec((1, TILE, TILE), lambda j, *_: (j, 0, 0)),
            ]
            + [whole(matrix.shape) for matrix in matrices],
            out_specs=[whole(shape) for shape in shapes],
            scratch_shapes=[pltpu.VMEM((chunk_total, 2, rows_padded, LANE), jnp.float32)],
        ),
        compiler_params=pltpu.CompilerParams(vmem_limit_bytes=VMEM_LIMIT),
        cost_estimate=pl.CostEstimate(
            flops=2 * 3 * rows_padded * TILE * tiles * TILE,
            bytes_accessed=8 * 1024 * 1024,
            transcendentals=0,
        ),
        name="fold_surface",
    )(jnp.asarray(chunk_table.reshape(-1)), field, flag, q, *matrices)


def exchange_plan(capacity, rows, stack, field, flag_t, q, first_row, row_taps, row_sums, table):
    chunk_table, chunk_total, atmos_cols = table
    reach = LON_REACH
    wide = atmos_cols + 2 * reach
    steps = -(-capacity // rows)
    tail = capacity - rows * (steps - 1)
    count = lambda t: tail if t == steps else rows

    around = {0: (0, rows)}
    pieces = {0: stack}
    for t in range(1, steps + 1):
        n = count(t)
        around[-t] = (-t * rows + rows - n, n)
        around[t] = (t * rows, n)
        pieces[-t] = shift(pieces[1 - t][:, rows - n :], "lat", 1)
        pieces[t] = shift(pieces[t - 1][:, :n], "lat", -1)
    order = sorted(around)
    matrices = {d: row_matrix(first_row - around[d][0], row_taps, around[d][1]) for d in order}

    *parts, ones = backward_call(
        field,
        flag_t,
        q,
        [matrices[d].T.astype(jnp.bfloat16) for d in order],
        chunk_table,
        chunk_total,
        wide,
    )

    def beside(start):
        edge = [part[:, :, start : start + reach] for part in parts]
        edge.append(jnp.broadcast_to(ones[None, :, start : start + reach], (2, 1, reach)))
        return jnp.concatenate(edge, axis=1)

    from_left = neighbour(beside(atmos_cols), "lon", 1)
    from_right = neighbour(beside(atmos_cols + reach), "lon", -1)
    width = parts[0].shape[2]

    def settle(part, row, n):
        low = from_left[:, row : row + n]
        high = from_right[:, row : row + n]
        rest = ((0, 0), (0, 0))
        return (
            part
            + jnp.pad(low, rest + ((0, width - reach),))
            + jnp.pad(high, rest + ((atmos_cols - reach, width - atmos_cols),))
        )

    totals, row = {}, 0
    for d, part in zip(order, parts):
        totals[d] = settle(part, row, part.shape[1])
        row += part.shape[1]
    lon_sums = settle(jnp.broadcast_to(ones[None], (2, 1, width)), row, 1)[0, 0, :atmos_cols]

    up, down = totals[steps], totals[-steps]
    for t in range(1, steps + 1):
        up, down = shift(up, "lat", 1), shift(down, "lat", -1)
        if t < steps:
            up = totals[steps - t] + jnp.pad(up, ((0, 0), (0, rows - up.shape[1]), (0, 0)))
            down = totals[t - steps] + jnp.pad(down, ((0, 0), (rows - down.shape[1], 0), (0, 0)))
    up = jnp.pad(up, ((0, 0), (0, rows - up.shape[1]), (0, 0)))
    down = jnp.pad(down, ((0, 0), (rows - down.shape[1], 0), (0, 0)))
    total = totals[0] + up + down

    ocean_flux = forward_call(
        [pieces[d] for d in order],
        [matrices[d].astype(jnp.bfloat16) for d in order],
        q,
        chunk_table,
        chunk_total,
        row_sums,
        flag_t,
    )
    lat_sums = total[1, :, wide]
    safe_surface = jnp.maximum(
        total[1, :, :atmos_cols], FLOOR_SHARE * (lat_sums[:, None] * lon_sums[None, :] + 1.0)
    )
    return ocean_flux, total[0, :, :atmos_cols] / safe_surface


def capacities_below(rows):
    return (rows, 2 * rows)


def local(
    exchange_density_arrays,
    marine_thermal_frozen_values,
    coarse_continent_flag,
    marine_continent_flag,
    parallel_source_initial,
    parallel_source_tally,
    parallel_intersect_coefs,
    meridian_source_displacement,
    meridian_source_tally,
    meridian_intersect_coefs,
):
    band_pos = lax.axis_index("lat")
    tile_pos = lax.axis_index("lon")
    bands = lax.axis_size("lat")
    atmos_rows, atmos_cols = coarse_continent_flag.shape
    ocean_rows, ocean_cols = marine_continent_flag.shape
    reach = LON_REACH
    chunk_table, chunk_total = tile_chunks(atmos_cols, ocean_cols)
    width = chunk_total * LANE

    water_atmos = (1 - coarse_continent_flag).astype(jnp.bfloat16)
    stack = jnp.concatenate(
        [exchange_density_arrays * water_atmos[None], water_atmos[None]], axis=0
    )
    channels = stack.shape[0]
    right = neighbour(stack[:, :, :reach], "lon", -1)
    left = neighbour(stack[:, :, atmos_cols - reach :], "lon", 1)
    filler = jnp.zeros((channels, atmos_rows, width - atmos_cols - 2 * reach), jnp.bfloat16)
    stack = jnp.concatenate([stack, right, left, filler], axis=2)

    here = lambda array, pos, count: lax.dynamic_slice_in_dim(array, pos * count, count)
    row_taps = tap_weights(
        here(parallel_source_tally, band_pos, ocean_rows),
        here(parallel_intersect_coefs, band_pos, ocean_rows),
    )
    col_taps = tap_weights(
        here(meridian_source_tally, tile_pos, ocean_cols),
        here(meridian_intersect_coefs, tile_pos, ocean_cols),
    )
    q = column_tiles(
        here(meridian_source_displacement, tile_pos, ocean_cols), col_taps, chunk_table, atmos_cols
    )
    row_sums = jnp.sum(row_taps, axis=1)[None, :]
    rows_padded = round_up(ocean_rows + 1, LANE)
    row_taps = jnp.pad(row_taps, ((0, rows_padded - ocean_rows), (0, 0)))
    first_row = here(parallel_source_initial, band_pos, ocean_rows) - band_pos * atmos_rows
    first_row = jnp.pad(first_row, (0, rows_padded - ocean_rows))

    starts = parallel_source_initial.reshape(bands, ocean_rows)
    band = jnp.arange(bands, dtype=jnp.int32)
    below = jnp.max(band * atmos_rows - starts[:, 0])
    above = jnp.max(starts[:, -1] + row_taps.shape[1] - (band + 1) * atmos_rows)
    need = jnp.maximum(below, above)
    longest = (bands - 1) * atmos_rows
    capacities = sorted({min(n, longest) for n in capacities_below(atmos_rows)} | {longest})
    choice = sum((need > n).astype(jnp.int32) for n in capacities[:-1])

    table = (chunk_table, chunk_total, atmos_cols)
    plans = [
        (lambda *operands, n=n: exchange_plan(n, atmos_rows, *operands, table)) for n in capacities
    ]
    ocean_flux, surface = lax.switch(
        choice,
        plans,
        stack,
        marine_thermal_frozen_values[0],
        marine_continent_flag.T,
        q,
        first_row,
        row_taps,
        row_sums,
    )
    return ocean_flux.transpose(0, 2, 1), surface[None]


def solution(mesh):
    fields = P(("group", "fld"), "lat", "lon")
    cells = P("lat", "lon")
    return jax.shard_map(
        local,
        mesh=mesh,
        in_specs=(fields, fields, cells, cells) + (P(),) * 6,
        out_specs=(fields, fields),
        check_vma=False,
    )
```

```python
import jax
import jax.numpy as jnp
import numpy as np
from jax import lax
from jax.experimental import pallas as pl
from jax.experimental.pallas import tpu as pltpu
from jax.sharding import PartitionSpec as P

LON_REACH = 4
FLOOR_SHARE = 0.25
TILE = 256
LANE = 128
VMEM_LIMIT = 56 * 1024 * 1024


def round_up(value, unit):
    return (value + unit - 1) // unit * unit


def neighbour(block, axis, step):
    count = lax.axis_size(axis)
    return lax.ppermute(block, axis, [(i, (i + step) % count) for i in range(count)])


def shift(block, axis, step):
    count = lax.axis_size(axis)
    pairs = [(i, i + step) for i in range(count) if 0 <= i + step < count]
    return lax.ppermute(block, axis, pairs)


def tap_weights(widths, weights):
    tap_count = weights.shape[1]
    allowed = jnp.arange(tap_count, dtype=jnp.int32)[None, :] < widths[:, None]
    return jnp.where(allowed, weights.astype(jnp.float32), jnp.float32(0.0))


def tile_chunks(atmos_cols, ocean_cols):
    tiles = -(-ocean_cols // TILE)
    chunk_total = round_up(atmos_cols + 2 * LON_REACH + 1, LANE) // LANE
    table = []
    for tile in range(tiles):
        first = tile * TILE
        last = min(first + TILE, ocean_cols) - 1
        slots = range(first // 3 - LON_REACH, last // 3 + LON_REACH + 1)
        chunks = sorted({(s if s >= 0 else atmos_cols + 2 * LON_REACH + s) // LANE for s in slots})
        assert len(chunks) <= 2
        if len(chunks) == 1:
            chunks.append((chunks[0] + 1) % chunk_total)
        table.append(chunks)
    return np.array(table, np.int32), chunk_total


def column_tiles(shift, col_taps, chunk_table, atmos_cols):
    tiles = chunk_table.shape[0]
    cols = shift.shape[0]
    pad = tiles * TILE - cols
    taps = jnp.pad(col_taps, ((0, pad), (0, 0))).T.reshape(-1, tiles, 1, TILE)
    first = jnp.arange(cols, dtype=jnp.int32) // 3 - LON_REACH + shift
    first = jnp.pad(first, (0, pad)).reshape(tiles, 1, TILE)
    slots = chunk_table[:, :, None] * LANE + np.arange(LANE)[None, None, :]
    slots = slots.reshape(tiles, TILE, 1)
    wide = atmos_cols + 2 * LON_REACH
    offset = np.where(slots < atmos_cols + LON_REACH, slots, np.where(slots < wide, slots - wide, -100))
    offset = jnp.asarray(offset.astype(np.int32))
    result = jnp.zeros((tiles, TILE, TILE), jnp.float32)
    for k in range(col_taps.shape[1]):
        result = result + jnp.where(offset == first + k, taps[k], jnp.float32(0.0))
    return result.astype(jnp.bfloat16)


def row_matrix(first_row, row_taps, atmos_total):
    index = jnp.arange(atmos_total, dtype=jnp.int32)[None, :]
    result = jnp.zeros((first_row.shape[0], atmos_total), jnp.float32)
    for k in range(row_taps.shape[1]):
        result = result + jnp.where(index == (first_row + k)[:, None], row_taps[:, k][:, None], 0.0)
    return result


def split(value):
    high = value.astype(jnp.bfloat16)
    low = (value - high.astype(jnp.float32)).astype(jnp.bfloat16)
    return high, low


def forward_kernel(blocks, chunk_ref, *refs):
    x_refs, p_refs = refs[:blocks], refs[blocks : 2 * blocks]
    q_ref, rows_ref, flag_ref, out_ref, high_ref, low_ref = refs[2 * blocks :]
    tile = pl.program_id(0)
    channels = x_refs[0].shape[0]
    chunk_total = high_ref.shape[0]
    ocean_rows = flag_ref.shape[1]

    @pl.when(tile == 0)
    def _():
        for ch in range(channels):
            value = None
            for x_ref, p_ref in zip(x_refs, p_refs):
                part = jnp.dot(p_ref[...], x_ref[ch], preferred_element_type=jnp.float32)
                value = part if value is None else value + part
            high, low = split(value.T)
            for c in range(chunk_total):
                high_ref[c, ch] = high[c * LANE : (c + 1) * LANE]
                low_ref[c, ch] = low[c * LANE : (c + 1) * LANE]

    first, second = chunk_ref[2 * tile], chunk_ref[2 * tile + 1]
    weights = q_ref[0].astype(jnp.float32).T
    col_sums = jnp.sum(weights, axis=1, keepdims=True)
    weights = weights.astype(jnp.bfloat16)

    def spread(ch):
        high = jnp.concatenate([high_ref[first, ch], high_ref[second, ch]], axis=0)
        low = jnp.concatenate([low_ref[first, ch], low_ref[second, ch]], axis=0)
        value = jnp.dot(weights, high, preferred_element_type=jnp.float32)
        value = value + jnp.dot(weights, low, preferred_element_type=jnp.float32)
        return value[:, :ocean_rows]

    floor = FLOOR_SHARE * rows_ref[...] * col_sums
    water = (1 - flag_ref[...]).astype(jnp.float32)
    factor = water / jnp.maximum(spread(channels - 1), floor)
    for ch in range(channels - 1):
        out_ref[ch] = (spread(ch) * factor).astype(out_ref.dtype)


def forward_call(pieces, matrices, q, chunk_table, chunk_total, row_sums, flag):
    blocks = len(pieces)
    channels = pieces[0].shape[0]
    rows_padded = matrices[0].shape[0]
    ocean_cols, ocean_rows = flag.shape
    tiles = q.shape[0]
    whole = lambda array: pl.BlockSpec(array.shape, lambda j, *_: (0,) * array.ndim)
    return pl.pallas_call(
        lambda *refs: forward_kernel(blocks, *refs),
        out_shape=jax.ShapeDtypeStruct((channels - 1, ocean_cols, ocean_rows), jnp.bfloat16),
        grid_spec=pltpu.PrefetchScalarGridSpec(
            num_scalar_prefetch=1,
            grid=(tiles,),
            in_specs=[whole(array) for array in (*pieces, *matrices)]
            + [
                pl.BlockSpec((1, TILE, TILE), lambda j, *_: (j, 0, 0)),
                whole(row_sums),
                pl.BlockSpec((TILE, ocean_rows), lambda j, *_: (j, 0)),
            ],
            out_specs=pl.BlockSpec((channels - 1, TILE, ocean_rows), lambda j, *_: (0, j, 0)),
            scratch_shapes=[
                pltpu.VMEM((chunk_total, channels, LANE, rows_padded), jnp.bfloat16),
                pltpu.VMEM((chunk_total, channels, LANE, rows_padded), jnp.bfloat16),
            ],
        ),
        compiler_params=pltpu.CompilerParams(vmem_limit_bytes=VMEM_LIMIT),
        cost_estimate=pl.CostEstimate(
            flops=2 * channels * rows_padded * 2 * TILE * tiles * TILE,
            bytes_accessed=16 * 1024 * 1024,
            transcendentals=0,
        ),
        name="spread_fluxes",
    )(jnp.asarray(chunk_table.reshape(-1)), *pieces, *matrices, q, row_sums, flag)


def backward_kernel(blocks, sizes, chunk_ref, field_ref, flag_ref, q_ref, *refs):
    ocean_rows, ocean_cols, wide = sizes
    matrix_refs, out_refs = refs[:blocks], refs[blocks : 2 * blocks]
    ones_ref, sum_ref = refs[2 * blocks :]
    tile = pl.program_id(0)
    chunk_total = sum_ref.shape[0]

    @pl.when(tile == 0)
    def _():
        lanes = lax.broadcasted_iota(jnp.int32, sum_ref.shape[1:], 2)
        for c in range(chunk_total):
            sum_ref[c] = jnp.where(lanes + c * LANE == wide, 1.0, 0.0)

    row = lax.broadcasted_iota(jnp.int32, field_ref.shape, 0)
    col = lax.broadcasted_iota(jnp.int32, field_ref.shape, 1)
    inside = col < ocean_cols - tile * TILE
    dry = flag_ref[...].astype(jnp.float32).T
    wet = inside & (row < ocean_rows) & (dry == 0.0)
    high, low = split(jnp.where(wet, field_ref[...], 0.0))
    water = jnp.where(wet | (inside & (row >= ocean_rows)), 1.0, 0.0).astype(jnp.bfloat16)
    weights = q_ref[0]

    def fold(value):
        return lax.dot_general(
            value, weights, (((1,), (1,)), ((), ())), preferred_element_type=jnp.float32
        )

    first, second = chunk_ref[2 * tile], chunk_ref[2 * tile + 1]
    for ch, value in enumerate((fold(high) + fold(low), fold(water))):
        sum_ref[first, ch] += value[:, :LANE]
        sum_ref[second, ch] += value[:, LANE:]

    @pl.when(tile == pl.num_programs(0) - 1)
    def _():
        for c in range(chunk_total):
            lanes = slice(c * LANE, (c + 1) * LANE)
            ones = sum_ref[c, 1, ocean_rows : ocean_rows + 1, :]
            ones_ref[:, lanes] = jnp.broadcast_to(ones, (8, LANE))
            for ch in range(2):
                high, low = split(sum_ref[c, ch])
                for matrix_ref, out_ref in zip(matrix_refs, out_refs):
                    matrix = matrix_ref[...]
                    total = jnp.dot(matrix, high, preferred_element_type=jnp.float32)
                    total = total + jnp.dot(matrix, low, preferred_element_type=jnp.float32)
                    out_ref[ch, :, lanes] = total


def backward_call(field, flag, q, matrices, chunk_table, chunk_total, wide):
    ocean_cols, ocean_rows = flag.shape
    rows_padded = matrices[0].shape[1]
    blocks = len(matrices)
    tiles = q.shape[0]
    width = chunk_total * LANE
    shapes = [(2, matrix.shape[0], width) for matrix in matrices] + [(8, width)]
    whole = lambda shape: pl.BlockSpec(shape, lambda j, *_: (0,) * len(shape))
    return pl.pallas_call(
        lambda *refs: backward_kernel(blocks, (ocean_rows, ocean_cols, wide), *refs),
        out_shape=[jax.ShapeDtypeStruct(shape, jnp.float32) for shape in shapes],
        grid_spec=pltpu.PrefetchScalarGridSpec(
            num_scalar_prefetch=1,
            grid=(tiles,),
            in_specs=[
                pl.BlockSpec((rows_padded, TILE), lambda j, *_: (0, j)),
                pl.BlockSpec((TILE, rows_padded), lambda j, *_: (j, 0)),
                pl.BlockSpec((1, TILE, TILE), lambda j, *_: (j, 0, 0)),
            ]
            + [whole(matrix.shape) for matrix in matrices],
            out_specs=[whole(shape) for shape in shapes],
            scratch_shapes=[pltpu.VMEM((chunk_total, 2, rows_padded, LANE), jnp.float32)],
        ),
        compiler_params=pltpu.CompilerParams(vmem_limit_bytes=VMEM_LIMIT),
        cost_estimate=pl.CostEstimate(
            flops=2 * 3 * rows_padded * TILE * tiles * TILE,
            bytes_accessed=8 * 1024 * 1024,
            transcendentals=0,
        ),
        name="fold_surface",
    )(jnp.asarray(chunk_table.reshape(-1)), field, flag, q, *matrices)


def neighbours_kernel(atmos_cols, stack_ref, to_left_ref, to_right_ref, *refs):
    part_refs, ones_ref = refs[:3], refs[3]
    own_ref, below_ref, above_ref, surface_ref = refs[4:8]
    (edge_left, edge_right, part_left, part_right, ones_left, ones_right) = refs[8:14]
    (total, sum_below, sum_above, x_send, x_recv, z_send, z_recv) = refs[14:]
    reach = LON_REACH
    wide = atmos_cols + 2 * reach
    width = stack_ref.shape[2]
    split_at = atmos_cols // LANE * LANE
    last = pl.ds(split_at, LANE)
    band, bands = lax.axis_index("lat"), lax.axis_size("lat")
    block, blocks = lax.axis_index("lon"), lax.axis_size("lon")
    left = {"lon": lax.rem(block + blocks - 1, blocks)}
    right = {"lon": lax.rem(block + 1, blocks)}
    has_above, has_below = band < bands - 1, band > 0
    above, below = {"lat": band + 1}, {"lat": band - 1}
    mesh_id = pl.DeviceIdType.MESH

    barrier = pltpu.get_barrier_semaphore()
    for target in (left, right):
        pl.semaphore_signal(barrier, inc=1, device_id=target, device_id_type=mesh_id)

    @pl.when(has_above)
    def _():
        pl.semaphore_signal(barrier, inc=1, device_id=above, device_id_type=mesh_id)

    @pl.when(has_below)
    def _():
        pl.semaphore_signal(barrier, inc=1, device_id=below, device_id_type=mesh_id)

    @pl.when(has_above & has_below)
    def _():
        pl.semaphore_wait(barrier, 4)

    @pl.when(jnp.logical_not(has_above & has_below))
    def _():
        pl.semaphore_wait(barrier, 3)

    def beside(slot, source, target, device):
        return pltpu.make_async_remote_copy(
            src_ref=source,
            dst_ref=target,
            send_sem=x_send.at[slot],
            recv_sem=x_recv.at[slot],
            device_id=device,
            device_id_type=mesh_id,
        )

    def upward(slot, source, target):
        return pltpu.make_async_remote_copy(
            src_ref=source,
            dst_ref=target,
            send_sem=z_send.at[slot],
            recv_sem=z_recv.at[slot],
            device_id=above,
            device_id_type=mesh_id,
        )

    def downward(slot, source, target):
        return pltpu.make_async_remote_copy(
            src_ref=source,
            dst_ref=target,
            send_sem=z_send.at[slot],
            recv_sem=z_recv.at[slot],
            device_id=below,
            device_id_type=mesh_id,
        )

    edges = [
        beside(0, to_left_ref, edge_right, left),
        beside(1, to_right_ref, edge_left, right),
    ]
    sums = []
    for i, part_ref in enumerate(part_refs):
        sums.append(beside(2 + 2 * i, part_ref.at[:, :, last], part_right.at[i], left))
        sums.append(beside(3 + 2 * i, part_ref.at[:, :, last], part_left.at[i], right))
    sums.append(beside(8, ones_ref.at[:, last], ones_right, left))
    sums.append(beside(9, ones_ref.at[:, last], ones_left, right))
    first = pl.ds(0, split_at)
    ups = [
        lambda: upward(0, stack_ref.at[:, :, first], below_ref.at[:, :, first]),
        lambda: upward(1, own_ref.at[:, :, last], below_ref.at[:, :, last]),
        lambda: upward(2, total.at[2], sum_below),
    ]
    downs = [
        lambda: downward(3, stack_ref.at[:, :, first], above_ref.at[:, :, first]),
        lambda: downward(4, own_ref.at[:, :, last], above_ref.at[:, :, last]),
        lambda: downward(5, total.at[0], sum_above),
    ]

    def start(i):
        @pl.when(has_above)
        def _():
            ups[i]().start()

        @pl.when(has_below)
        def _():
            downs[i]().start()

    for copy in edges + sums:
        copy.start()
    start(0)

    @pl.when(band == 0)
    def _():
        below_ref[...] = jnp.zeros_like(below_ref)
        sum_below[...] = jnp.zeros_like(sum_below)

    @pl.when(band == bands - 1)
    def _():
        above_ref[...] = jnp.zeros_like(above_ref)
        sum_above[...] = jnp.zeros_like(sum_above)

    for copy in edges:
        copy.wait()
    for ch in range(stack_ref.shape[0]):
        own_ref[ch, :, :split_at] = stack_ref[ch, :, :split_at]
        own_ref[ch, :, split_at:] = (
            stack_ref[ch, :, split_at:].astype(jnp.float32)
            + edge_left[ch].astype(jnp.float32)
            + edge_right[ch].astype(jnp.float32)
        ).astype(jnp.bfloat16)
    start(1)

    for copy in sums:
        copy.wait()
    at = atmos_cols - split_at

    def settle(value, from_left, from_right):
        lane = lax.broadcasted_iota(jnp.int32, from_left.shape, 1)
        low = jnp.where(lane < reach, pltpu.roll(from_left, LANE - at, 1), 0.0)
        mine = (lane >= at - reach) & (lane < at)
        high = jnp.where(mine, pltpu.roll(from_right, LANE - 2 * reach, 1), 0.0)
        if split_at == 0:
            return value + low + high
        middle = [value[:, LANE:split_at]] if split_at > LANE else []
        return jnp.concatenate(
            [value[:, :LANE] + low, *middle, value[:, split_at:] + high], axis=1
        )

    for i in (0, 2, 1):
        for ch in range(2):
            total[i, ch] = settle(part_refs[i][ch], part_left[i, ch], part_right[i, ch])
        if i == 2:
            start(2)
    lon_sums = settle(ones_ref[...], ones_left[...], ones_right[...])[:1]

    @pl.when(has_below)
    def _():
        ups[2]().wait_recv()

    @pl.when(has_above)
    def _():
        downs[2]().wait_recv()

    value = [total[1, ch] + sum_below[ch] + sum_above[ch] for ch in range(2)]
    lat_sums = value[1][:, wide : wide + 1]
    safe = jnp.maximum(value[1], FLOOR_SHARE * (lat_sums * lon_sums + 1.0))
    surface_ref[...] = value[0] / safe

    for i in range(2):

        @pl.when(has_below)
        def _():
            ups[i]().wait_recv()

        @pl.when(has_above)
        def _():
            downs[i]().wait_recv()

    for i in range(3):

        @pl.when(has_above)
        def _():
            ups[i]().wait_send()

        @pl.when(has_below)
        def _():
            downs[i]().wait_send()


def neighbours_call(stack, to_left, to_right, parts, ones, atmos_cols):
    channels, rows, width = stack.shape
    vmem = pl.BlockSpec(memory_space=pltpu.VMEM)
    edge = pltpu.VMEM((channels, rows, LANE), jnp.bfloat16)
    beside = pltpu.VMEM((3, 2, rows, LANE), jnp.float32)
    column = pltpu.VMEM((8, LANE), jnp.float32)
    block = pltpu.VMEM((2, rows, width), jnp.float32)
    return pl.pallas_call(
        lambda *refs: neighbours_kernel(atmos_cols, *refs),
        out_shape=[jax.ShapeDtypeStruct(stack.shape, stack.dtype)] * 3
        + [jax.ShapeDtypeStruct((rows, width), jnp.float32)],
        in_specs=[vmem] * 7,
        out_specs=[vmem] * 4,
        scratch_shapes=[
            edge,
            edge,
            beside,
            beside,
            column,
            column,
            pltpu.VMEM((3, 2, rows, width), jnp.float32),
            block,
            block,
            pltpu.SemaphoreType.DMA((10,)),
            pltpu.SemaphoreType.DMA((10,)),
            pltpu.SemaphoreType.DMA((6,)),
            pltpu.SemaphoreType.DMA((6,)),
        ],
        compiler_params=pltpu.CompilerParams(
            collective_id=0, has_side_effects=True, vmem_limit_bytes=VMEM_LIMIT
        ),
        name="exchange_neighbours",
    )(stack, to_left, to_right, *parts, ones)


def neighbours_plan(rows, stack, field, flag_t, q, first_row, row_taps, row_sums, table):
    chunk_table, chunk_total, atmos_cols = table
    reach = LON_REACH
    at = atmos_cols % LANE
    assert reach <= at and at + 2 * reach < LANE
    place = lambda edge, lane: jnp.pad(edge, ((0, 0), (0, 0), (lane, LANE - reach - lane)))
    to_left = place(stack[:, :, :reach], at)
    to_right = place(stack[:, :, atmos_cols - reach : atmos_cols], at + reach)
    matrices = [row_matrix(first_row + d * rows, row_taps, rows) for d in (1, 0, -1)]
    *parts, ones = backward_call(
        field,
        flag_t,
        q,
        [matrix.T.astype(jnp.bfloat16) for matrix in matrices],
        chunk_table,
        chunk_total,
        atmos_cols + 2 * reach,
    )
    own, below, above, surface = neighbours_call(stack, to_left, to_right, parts, ones, atmos_cols)
    ocean_flux = forward_call(
        [below, own, above],
        [matrix.astype(jnp.bfloat16) for matrix in matrices],
        q,
        chunk_table,
        chunk_total,
        row_sums,
        flag_t,
    )
    return ocean_flux, surface[:, :atmos_cols]


def exchange_plan(capacity, rows, stack, field, flag_t, q, first_row, row_taps, row_sums, table):
    chunk_table, chunk_total, atmos_cols = table
    reach = LON_REACH
    wide = atmos_cols + 2 * reach
    steps = -(-capacity // rows)
    tail = capacity - rows * (steps - 1)
    count = lambda t: tail if t == steps else rows

    right = neighbour(stack[:, :, :reach], "lon", -1)
    left = neighbour(stack[:, :, atmos_cols - reach : atmos_cols], "lon", 1)
    filler = jnp.zeros(stack.shape[:2] + (stack.shape[2] - wide,), stack.dtype)
    stack = jnp.concatenate([stack[:, :, :atmos_cols], right, left, filler], axis=2)

    around = {0: (0, rows)}
    pieces = {0: stack}
    for t in range(1, steps + 1):
        n = count(t)
        around[-t] = (-t * rows + rows - n, n)
        around[t] = (t * rows, n)
        pieces[-t] = shift(pieces[1 - t][:, rows - n :], "lat", 1)
        pieces[t] = shift(pieces[t - 1][:, :n], "lat", -1)
    order = sorted(around)
    matrices = {d: row_matrix(first_row - around[d][0], row_taps, around[d][1]) for d in order}

    *parts, ones = backward_call(
        field,
        flag_t,
        q,
        [matrices[d].T.astype(jnp.bfloat16) for d in order],
        chunk_table,
        chunk_total,
        wide,
    )

    def beside(start):
        edge = [part[:, :, start : start + reach] for part in parts]
        edge.append(jnp.broadcast_to(ones[None, :1, start : start + reach], (2, 1, reach)))
        return jnp.concatenate(edge, axis=1)

    from_left = neighbour(beside(atmos_cols), "lon", 1)
    from_right = neighbour(beside(atmos_cols + reach), "lon", -1)
    width = parts[0].shape[2]

    def settle(part, row, n):
        low = from_left[:, row : row + n]
        high = from_right[:, row : row + n]
        rest = ((0, 0), (0, 0))
        return (
            part
            + jnp.pad(low, rest + ((0, width - reach),))
            + jnp.pad(high, rest + ((atmos_cols - reach, width - atmos_cols),))
        )

    totals, row = {}, 0
    for d, part in zip(order, parts):
        totals[d] = settle(part, row, part.shape[1])
        row += part.shape[1]
    lon_sums = settle(jnp.broadcast_to(ones[None, :1], (2, 1, width)), row, 1)[0, 0, :atmos_cols]

    up, down = totals[steps], totals[-steps]
    for t in range(1, steps + 1):
        up, down = shift(up, "lat", 1), shift(down, "lat", -1)
        if t < steps:
            up = totals[steps - t] + jnp.pad(up, ((0, 0), (0, rows - up.shape[1]), (0, 0)))
            down = totals[t - steps] + jnp.pad(down, ((0, 0), (rows - down.shape[1], 0), (0, 0)))
    up = jnp.pad(up, ((0, 0), (0, rows - up.shape[1]), (0, 0)))
    down = jnp.pad(down, ((0, 0), (rows - down.shape[1], 0), (0, 0)))
    total = totals[0] + up + down

    ocean_flux = forward_call(
        [pieces[d] for d in order],
        [matrices[d].astype(jnp.bfloat16) for d in order],
        q,
        chunk_table,
        chunk_total,
        row_sums,
        flag_t,
    )
    lat_sums = total[1, :, wide]
    safe_surface = jnp.maximum(
        total[1, :, :atmos_cols], FLOOR_SHARE * (lat_sums[:, None] * lon_sums[None, :] + 1.0)
    )
    return ocean_flux, total[0, :, :atmos_cols] / safe_surface


def capacities_below(rows):
    return (rows, 2 * rows)


def local(
    exchange_density_arrays,
    marine_thermal_frozen_values,
    coarse_continent_flag,
    marine_continent_flag,
    parallel_source_initial,
    parallel_source_tally,
    parallel_intersect_coefs,
    meridian_source_displacement,
    meridian_source_tally,
    meridian_intersect_coefs,
):
    band_pos = lax.axis_index("lat")
    tile_pos = lax.axis_index("lon")
    bands = lax.axis_size("lat")
    atmos_rows, atmos_cols = coarse_continent_flag.shape
    ocean_rows, ocean_cols = marine_continent_flag.shape
    reach = LON_REACH
    chunk_table, chunk_total = tile_chunks(atmos_cols, ocean_cols)
    width = chunk_total * LANE

    water_atmos = (1 - coarse_continent_flag).astype(jnp.bfloat16)
    stack = jnp.concatenate(
        [exchange_density_arrays * water_atmos[None], water_atmos[None]], axis=0
    )
    stack = jnp.pad(stack, ((0, 0), (0, 0), (0, width - atmos_cols)))

    here = lambda array, pos, count: lax.dynamic_slice_in_dim(array, pos * count, count)
    row_taps = tap_weights(
        here(parallel_source_tally, band_pos, ocean_rows),
        here(parallel_intersect_coefs, band_pos, ocean_rows),
    )
    col_taps = tap_weights(
        here(meridian_source_tally, tile_pos, ocean_cols),
        here(meridian_intersect_coefs, tile_pos, ocean_cols),
    )
    q = column_tiles(
        here(meridian_source_displacement, tile_pos, ocean_cols), col_taps, chunk_table, atmos_cols
    )
    row_sums = jnp.sum(row_taps, axis=1)[None, :]
    rows_padded = round_up(ocean_rows + 1, LANE)
    row_taps = jnp.pad(row_taps, ((0, rows_padded - ocean_rows), (0, 0)))
    first_row = here(parallel_source_initial, band_pos, ocean_rows) - band_pos * atmos_rows
    first_row = jnp.pad(first_row, (0, rows_padded - ocean_rows))

    starts = parallel_source_initial.reshape(bands, ocean_rows)
    band = jnp.arange(bands, dtype=jnp.int32)
    below = jnp.max(band * atmos_rows - starts[:, 0])
    above = jnp.max(starts[:, -1] + row_taps.shape[1] - (band + 1) * atmos_rows)
    need = jnp.maximum(below, above)
    longest = (bands - 1) * atmos_rows
    capacities = sorted({min(n, longest) for n in capacities_below(atmos_rows)} | {longest})
    choice = sum((need > n).astype(jnp.int32) for n in capacities[:-1])

    table = (chunk_table, chunk_total, atmos_cols)
    plans = [
        (lambda *operands, n=n: exchange_plan(n, atmos_rows, *operands, table)) for n in capacities
    ]
    plans[0] = lambda *operands: neighbours_plan(atmos_rows, *operands, table)
    ocean_flux, surface = lax.switch(
        choice,
        plans,
        stack,
        marine_thermal_frozen_values[0],
        marine_continent_flag.T,
        q,
        first_row,
        row_taps,
        row_sums,
    )
    return ocean_flux.transpose(0, 2, 1), surface[None]


def solution(mesh):
    fields = P(("group", "fld"), "lat", "lon")
    cells = P("lat", "lon")
    return jax.shard_map(
        local,
        mesh=mesh,
        in_specs=(fields, fields, cells, cells) + (P(),) * 6,
        out_specs=(fields, fields),
        check_vma=False,
    )
```

```python
import jax
import jax.numpy as jnp
import numpy as np
from jax import lax
from jax.experimental import pallas as pl
from jax.experimental.layout import Layout, with_layout_constraint
from jax.experimental.pallas import tpu as pltpu
from jax.sharding import PartitionSpec as P

LON_REACH = 4
FLOOR_SHARE = 0.25
TILE = 256
LANE = 128
VMEM_LIMIT = 56 * 1024 * 1024


def round_up(value, unit):
    return (value + unit - 1) // unit * unit


def neighbour(block, axis, step):
    count = lax.axis_size(axis)
    return lax.ppermute(block, axis, [(i, (i + step) % count) for i in range(count)])


def shift(block, axis, step):
    count = lax.axis_size(axis)
    pairs = [(i, i + step) for i in range(count) if 0 <= i + step < count]
    return lax.ppermute(block, axis, pairs)


def tap_weights(widths, weights):
    tap_count = weights.shape[1]
    allowed = jnp.arange(tap_count, dtype=jnp.int32)[None, :] < widths[:, None]
    return jnp.where(allowed, weights.astype(jnp.float32), jnp.float32(0.0))


def tile_chunks(atmos_cols, ocean_cols):
    tiles = -(-ocean_cols // TILE)
    chunk_total = round_up(atmos_cols + 2 * LON_REACH + 1, LANE) // LANE
    table = []
    for tile in range(tiles):
        first = tile * TILE
        last = min(first + TILE, ocean_cols) - 1
        slots = range(first // 3 - LON_REACH, last // 3 + LON_REACH + 1)
        chunks = sorted({(s if s >= 0 else atmos_cols + 2 * LON_REACH + s) // LANE for s in slots})
        assert len(chunks) <= 2
        if len(chunks) == 1:
            chunks.append((chunks[0] + 1) % chunk_total)
        table.append(chunks)
    return np.array(table, np.int32), chunk_total


def column_tiles(shift, col_taps, chunk_table, atmos_cols):
    tiles = chunk_table.shape[0]
    cols = shift.shape[0]
    pad = tiles * TILE - cols
    taps = jnp.pad(col_taps, ((0, pad), (0, 0))).T.reshape(-1, tiles, 1, TILE)
    first = jnp.arange(cols, dtype=jnp.int32) // 3 - LON_REACH + shift
    first = jnp.pad(first, (0, pad)).reshape(tiles, 1, TILE)
    slots = chunk_table[:, :, None] * LANE + np.arange(LANE)[None, None, :]
    slots = slots.reshape(tiles, TILE, 1)
    wide = atmos_cols + 2 * LON_REACH
    offset = np.where(slots < atmos_cols + LON_REACH, slots, np.where(slots < wide, slots - wide, -100))
    offset = jnp.asarray(offset.astype(np.int32))
    result = jnp.zeros((tiles, TILE, TILE), jnp.float32)
    for k in range(col_taps.shape[1]):
        result = result + jnp.where(offset == first + k, taps[k], jnp.float32(0.0))
    return result.astype(jnp.bfloat16)


def row_matrix(first_row, row_taps, atmos_total):
    index = jnp.arange(atmos_total, dtype=jnp.int32)[None, :]
    result = jnp.zeros((first_row.shape[0], atmos_total), jnp.float32)
    for k in range(row_taps.shape[1]):
        result = result + jnp.where(index == (first_row + k)[:, None], row_taps[:, k][:, None], 0.0)
    return result


def split(value):
    high = value.astype(jnp.bfloat16)
    low = (value - high.astype(jnp.float32)).astype(jnp.bfloat16)
    return high, low


def forward_kernel(blocks, chunk_ref, *refs):
    x_refs, p_refs = refs[:blocks], refs[blocks : 2 * blocks]
    q_ref, rows_ref, flag_ref, out_ref, high_ref, low_ref = refs[2 * blocks :]
    tile = pl.program_id(0)
    channels = x_refs[0].shape[0]
    chunk_total = high_ref.shape[0]
    ocean_rows = flag_ref.shape[1]

    @pl.when(tile == 0)
    def _():
        for ch in range(channels):
            value = None
            for x_ref, p_ref in zip(x_refs, p_refs):
                part = jnp.dot(p_ref[...], x_ref[ch], preferred_element_type=jnp.float32)
                value = part if value is None else value + part
            high, low = split(value.T)
            for c in range(chunk_total):
                high_ref[c, ch] = high[c * LANE : (c + 1) * LANE]
                low_ref[c, ch] = low[c * LANE : (c + 1) * LANE]

    first, second = chunk_ref[2 * tile], chunk_ref[2 * tile + 1]
    weights = q_ref[0].astype(jnp.float32).T
    col_sums = jnp.sum(weights, axis=1, keepdims=True)
    weights = weights.astype(jnp.bfloat16)

    def spread(ch):
        high = jnp.concatenate([high_ref[first, ch], high_ref[second, ch]], axis=0)
        low = jnp.concatenate([low_ref[first, ch], low_ref[second, ch]], axis=0)
        value = jnp.dot(weights, high, preferred_element_type=jnp.float32)
        value = value + jnp.dot(weights, low, preferred_element_type=jnp.float32)
        return value[:, :ocean_rows]

    floor = FLOOR_SHARE * rows_ref[...] * col_sums
    water = (1 - flag_ref[...]).astype(jnp.float32)
    factor = water / jnp.maximum(spread(channels - 1), floor)
    for ch in range(channels - 1):
        out_ref[ch] = (spread(ch) * factor).astype(out_ref.dtype)


def forward_call(pieces, matrices, q, chunk_table, chunk_total, row_sums, flag):
    blocks = len(pieces)
    channels = pieces[0].shape[0]
    rows_padded = matrices[0].shape[0]
    ocean_cols, ocean_rows = flag.shape
    tiles = q.shape[0]
    whole = lambda array: pl.BlockSpec(array.shape, lambda j, *_: (0,) * array.ndim)
    return pl.pallas_call(
        lambda *refs: forward_kernel(blocks, *refs),
        out_shape=jax.ShapeDtypeStruct((channels - 1, ocean_cols, ocean_rows), jnp.bfloat16),
        grid_spec=pltpu.PrefetchScalarGridSpec(
            num_scalar_prefetch=1,
            grid=(tiles,),
            in_specs=[whole(array) for array in (*pieces, *matrices)]
            + [
                pl.BlockSpec((1, TILE, TILE), lambda j, *_: (j, 0, 0)),
                whole(row_sums),
                pl.BlockSpec((TILE, ocean_rows), lambda j, *_: (j, 0)),
            ],
            out_specs=pl.BlockSpec((channels - 1, TILE, ocean_rows), lambda j, *_: (0, j, 0)),
            scratch_shapes=[
                pltpu.VMEM((chunk_total, channels, LANE, rows_padded), jnp.bfloat16),
                pltpu.VMEM((chunk_total, channels, LANE, rows_padded), jnp.bfloat16),
            ],
        ),
        compiler_params=pltpu.CompilerParams(vmem_limit_bytes=VMEM_LIMIT),
        cost_estimate=pl.CostEstimate(
            flops=2 * channels * rows_padded * 2 * TILE * tiles * TILE,
            bytes_accessed=16 * 1024 * 1024,
            transcendentals=0,
        ),
        name="spread_fluxes",
    )(jnp.asarray(chunk_table.reshape(-1)), *pieces, *matrices, q, row_sums, flag)


def backward_kernel(blocks, sizes, chunk_ref, field_ref, flag_ref, q_ref, *refs):
    ocean_rows, ocean_cols, wide = sizes
    matrix_refs, out_refs = refs[:blocks], refs[blocks : 2 * blocks]
    ones_ref, sum_ref = refs[2 * blocks :]
    tile = pl.program_id(0)
    chunk_total = sum_ref.shape[0]

    @pl.when(tile == 0)
    def _():
        lanes = lax.broadcasted_iota(jnp.int32, sum_ref.shape[1:], 2)
        for c in range(chunk_total):
            sum_ref[c] = jnp.where(lanes + c * LANE == wide, 1.0, 0.0)

    row = lax.broadcasted_iota(jnp.int32, field_ref.shape, 0)
    col = lax.broadcasted_iota(jnp.int32, field_ref.shape, 1)
    inside = col < ocean_cols - tile * TILE
    dry = flag_ref[...].astype(jnp.float32).T
    wet = inside & (row < ocean_rows) & (dry == 0.0)
    high, low = split(jnp.where(wet, field_ref[...], 0.0))
    water = jnp.where(wet | (inside & (row >= ocean_rows)), 1.0, 0.0).astype(jnp.bfloat16)
    weights = q_ref[0]

    def fold(value):
        return lax.dot_general(
            value, weights, (((1,), (1,)), ((), ())), preferred_element_type=jnp.float32
        )

    first, second = chunk_ref[2 * tile], chunk_ref[2 * tile + 1]
    for ch, value in enumerate((fold(high) + fold(low), fold(water))):
        sum_ref[first, ch] += value[:, :LANE]
        sum_ref[second, ch] += value[:, LANE:]

    @pl.when(tile == pl.num_programs(0) - 1)
    def _():
        for c in range(chunk_total):
            lanes = slice(c * LANE, (c + 1) * LANE)
            ones = sum_ref[c, 1, ocean_rows : ocean_rows + 1, :]
            ones_ref[:, lanes] = jnp.broadcast_to(ones, (8, LANE))
            for ch in range(2):
                high, low = split(sum_ref[c, ch])
                for matrix_ref, out_ref in zip(matrix_refs, out_refs):
                    matrix = matrix_ref[...]
                    total = jnp.dot(matrix, high, preferred_element_type=jnp.float32)
                    total = total + jnp.dot(matrix, low, preferred_element_type=jnp.float32)
                    out_ref[ch, :, lanes] = total


def backward_call(field, flag, q, matrices, chunk_table, chunk_total, wide):
    ocean_cols, ocean_rows = flag.shape
    rows_padded = matrices[0].shape[1]
    blocks = len(matrices)
    tiles = q.shape[0]
    width = chunk_total * LANE
    shapes = [(2, matrix.shape[0], width) for matrix in matrices] + [(8, width)]
    whole = lambda shape: pl.BlockSpec(shape, lambda j, *_: (0,) * len(shape))
    return pl.pallas_call(
        lambda *refs: backward_kernel(blocks, (ocean_rows, ocean_cols, wide), *refs),
        out_shape=[jax.ShapeDtypeStruct(shape, jnp.float32) for shape in shapes],
        grid_spec=pltpu.PrefetchScalarGridSpec(
            num_scalar_prefetch=1,
            grid=(tiles,),
            in_specs=[
                pl.BlockSpec((rows_padded, TILE), lambda j, *_: (0, j)),
                pl.BlockSpec((TILE, rows_padded), lambda j, *_: (j, 0)),
                pl.BlockSpec((1, TILE, TILE), lambda j, *_: (j, 0, 0)),
            ]
            + [whole(matrix.shape) for matrix in matrices],
            out_specs=[whole(shape) for shape in shapes],
            scratch_shapes=[pltpu.VMEM((chunk_total, 2, rows_padded, LANE), jnp.float32)],
        ),
        compiler_params=pltpu.CompilerParams(vmem_limit_bytes=VMEM_LIMIT),
        cost_estimate=pl.CostEstimate(
            flops=2 * 3 * rows_padded * TILE * tiles * TILE,
            bytes_accessed=8 * 1024 * 1024,
            transcendentals=0,
        ),
        name="fold_surface",
    )(jnp.asarray(chunk_table.reshape(-1)), field, flag, q, *matrices)


def neighbours_kernel(steps, chunk_table, flux_ref, land_ref, field_ref, flag_ref, q_ref, *refs):
    blocks_here = 2 * steps + 1
    matrix_refs, piece_refs = refs[:blocks_here], refs[blocks_here : 2 * blocks_here]
    surface_ref, *refs = refs[2 * blocks_here :]
    (edge_left, edge_right, part_left, part_right, ones_left, ones_right) = refs[:6]
    (folded, part, ones_ref, total, sum_below, sum_above) = refs[6:12]
    (x_send, x_recv, z_send, z_recv) = refs[12:]
    own_ref = piece_refs[steps]
    reach = LON_REACH
    channels, atmos_rows, atmos_cols = flux_ref.shape
    channels += 1
    ocean_rows, ocean_cols = field_ref.shape
    wide = atmos_cols + 2 * reach
    width = own_ref.shape[2]
    split_at = atmos_cols // LANE * LANE
    last = pl.ds(split_at, LANE)
    band, bands = lax.axis_index("lat"), lax.axis_size("lat")
    block, blocks = lax.axis_index("lon"), lax.axis_size("lon")
    left = {"lon": lax.rem(block + blocks - 1, blocks)}
    right = {"lon": lax.rem(block + 1, blocks)}
    has_above, has_below = band < bands - 1, band > 0
    above, below = {"lat": band + 1}, {"lat": band - 1}
    mesh_id = pl.DeviceIdType.MESH

    water_atmos = (1 - land_ref[...]).astype(jnp.float32)
    for ch in range(channels):
        value = water_atmos
        if ch < channels - 1:
            value = value * flux_ref[ch].astype(jnp.float32)
        own_ref[ch, :, last] = jnp.zeros((atmos_rows, LANE), jnp.bfloat16)
        own_ref[ch, :, :atmos_cols] = value.astype(jnp.bfloat16)

    barrier = pltpu.get_barrier_semaphore()
    for target in (left, right):
        pl.semaphore_signal(barrier, inc=1, device_id=target, device_id_type=mesh_id)

    @pl.when(has_above)
    def _():
        pl.semaphore_signal(barrier, inc=1, device_id=above, device_id_type=mesh_id)

    @pl.when(has_below)
    def _():
        pl.semaphore_signal(barrier, inc=1, device_id=below, device_id_type=mesh_id)

    @pl.when(has_above & has_below)
    def _():
        pl.semaphore_wait(barrier, 4)

    @pl.when(jnp.logical_not(has_above & has_below))
    def _():
        pl.semaphore_wait(barrier, 3)

    def beside(slot, source, target, device):
        return pltpu.make_async_remote_copy(
            src_ref=source,
            dst_ref=target,
            send_sem=x_send.at[slot],
            recv_sem=x_recv.at[slot],
            device_id=device,
            device_id_type=mesh_id,
        )

    def upward(slot, source, target):
        return pltpu.make_async_remote_copy(
            src_ref=source,
            dst_ref=target,
            send_sem=z_send.at[slot],
            recv_sem=z_recv.at[slot],
            device_id=above,
            device_id_type=mesh_id,
        )

    def downward(slot, source, target):
        return pltpu.make_async_remote_copy(
            src_ref=source,
            dst_ref=target,
            send_sem=z_send.at[slot],
            recv_sem=z_recv.at[slot],
            device_id=below,
            device_id_type=mesh_id,
        )

    edges = [
        beside(0, own_ref.at[:, :, pl.ds(0, LANE)], edge_right, left),
        beside(1, own_ref.at[:, :, last], edge_left, right),
    ]
    sums = []
    for i in range(blocks_here):
        sums.append(beside(2 + 2 * i, part.at[i, :, :, last], part_right.at[i], left))
        sums.append(beside(3 + 2 * i, part.at[i, :, :, last], part_left.at[i], right))
    sums.append(beside(2 * blocks_here + 2, ones_ref.at[:, last], ones_right, left))
    sums.append(beside(2 * blocks_here + 3, ones_ref.at[:, last], ones_left, right))
    first = pl.ds(0, split_at)
    ups, downs = [], []
    for t in range(steps):
        source, target = piece_refs[steps - t], piece_refs[steps - t - 1]
        for part_of, columns in enumerate((first, last)):
            ups.append((3 * t + part_of, source.at[:, :, columns], target.at[:, :, columns]))
        ups.append((3 * t + 2, total.at[2 * steps - t], sum_below.at[t]))
        source, target = piece_refs[steps + t], piece_refs[steps + t + 1]
        for part_of, columns in enumerate((first, last)):
            slot = 3 * (steps + t) + part_of
            downs.append((slot, source.at[:, :, columns], target.at[:, :, columns]))
        downs.append((3 * (steps + t) + 2, total.at[t], sum_above.at[t]))

    def start(i):
        @pl.when(has_above)
        def _():
            upward(*ups[i]).start()

        @pl.when(has_below)
        def _():
            downward(*downs[i]).start()

    def arrive(i):
        @pl.when(has_below)
        def _():
            upward(*ups[i]).wait_recv()

        @pl.when(has_above)
        def _():
            downward(*downs[i]).wait_recv()

    for copy in edges:
        copy.start()
    start(0)

    @pl.when(band == 0)
    def _():
        for piece_ref in piece_refs[:steps]:
            piece_ref[...] = jnp.zeros_like(piece_ref)
        sum_below[...] = jnp.zeros_like(sum_below)

    @pl.when(band == bands - 1)
    def _():
        for piece_ref in piece_refs[steps + 1 :]:
            piece_ref[...] = jnp.zeros_like(piece_ref)
        sum_above[...] = jnp.zeros_like(sum_above)

    for copy in edges:
        copy.wait()
    at = atmos_cols - split_at
    lane = lax.broadcasted_iota(jnp.int32, (atmos_rows, LANE), 1)
    for ch in range(channels):
        value = own_ref[ch, :, last].astype(jnp.float32)
        from_right = pltpu.roll(edge_right[ch].astype(jnp.float32), at, 1)
        from_left = pltpu.roll(edge_left[ch].astype(jnp.float32), 2 * reach, 1)
        value = jnp.where((lane >= at) & (lane < at + reach), from_right, value)
        value = jnp.where((lane >= at + reach) & (lane < at + 2 * reach), from_left, value)
        own_ref[ch, :, last] = value.astype(jnp.bfloat16)
    start(1)

    lanes = lax.broadcasted_iota(jnp.int32, folded.shape[1:], 2)
    for c in range(folded.shape[0]):
        folded[c] = jnp.where(lanes + c * LANE == wide, 1.0, 0.0)
    ones_ref[...] = jnp.zeros_like(ones_ref)
    for tile, (low_chunk, high_chunk) in enumerate(chunk_table):
        cols = slice(tile * TILE, min((tile + 1) * TILE, ocean_cols))
        weights = q_ref[tile][:, : cols.stop - cols.start]

        def fold(value):
            return lax.dot_general(
                value, weights, (((1,), (1,)), ((), ())), preferred_element_type=jnp.float32
            )

        water = (1 - flag_ref[cols, :]).astype(jnp.float32).T
        high, low = split(field_ref[:, cols] * water)
        sums_of = [fold(high) + fold(low), fold(water.astype(jnp.bfloat16))]
        for ch in range(2):
            folded[low_chunk, ch] += sums_of[ch][:, :LANE]
            folded[high_chunk, ch] += sums_of[ch][:, LANE:]
        value = fold(jnp.ones((8, cols.stop - cols.start), jnp.bfloat16))
        for half, c in enumerate((low_chunk, high_chunk)):
            at_chunk = slice(c * LANE, (c + 1) * LANE)
            ones_ref[:, at_chunk] += value[:, half * LANE : (half + 1) * LANE]
    for c in range(folded.shape[0]):
        at_chunk = slice(c * LANE, (c + 1) * LANE)
        for ch in range(2):
            high, low = split(folded[c, ch])
            for i, matrix_ref in enumerate(matrix_refs):
                value = jnp.dot(matrix_ref[...], high, preferred_element_type=jnp.float32)
                value = value + jnp.dot(matrix_ref[...], low, preferred_element_type=jnp.float32)
                part[i, ch, :, at_chunk] = value
    for copy in sums:
        copy.start()
    for i in range(3, 3 * steps):
        if i % 3 < 2:
            arrive(i - 3)
            start(i)

    for copy in sums:
        copy.wait()

    def settle(value, from_left, from_right):
        lane = lax.broadcasted_iota(jnp.int32, from_left.shape, 1)
        low = jnp.where(lane < reach, pltpu.roll(from_left, LANE - at, 1), 0.0)
        mine = (lane >= at - reach) & (lane < at)
        high = jnp.where(mine, pltpu.roll(from_right, LANE - 2 * reach, 1), 0.0)
        if split_at == 0:
            return value + low + high
        middle = [value[:, LANE:split_at]] if split_at > LANE else []
        return jnp.concatenate(
            [value[:, :LANE] + low, *middle, value[:, split_at:] + high], axis=1
        )

    for i in sorted(range(blocks_here), key=lambda i: -abs(i - steps)):
        for ch in range(2):
            total[i, ch] = settle(part[i, ch], part_left[i, ch], part_right[i, ch])
        if i == 2 * steps:
            start(2)
    lon_sums = settle(ones_ref[...], ones_left[...], ones_right[...])[:1]

    for t in range(1, steps):
        arrive(3 * t - 1)
        total[2 * steps - t] += sum_below[t - 1]
        total[t] += sum_above[t - 1]
        start(3 * t + 2)
    arrive(3 * steps - 1)

    value = [
        total[steps, ch] + sum_below[steps - 1, ch] + sum_above[steps - 1, ch] for ch in range(2)
    ]
    lat_sums = value[1][:, wide : wide + 1]
    safe = jnp.maximum(value[1], FLOOR_SHARE * (lat_sums * lon_sums + 1.0))
    surface_ref[...] = value[0] / safe

    for i in (3 * steps - 3, 3 * steps - 2):
        arrive(i)

    for i in range(3 * steps):

        @pl.when(has_above)
        def _():
            upward(*ups[i]).wait_send()

        @pl.when(has_below)
        def _():
            downward(*downs[i]).wait_send()


def neighbours_call(fluxes, land, field, flag_t, q, matrices, chunk_table, chunk_total):
    fields, rows, atmos_cols = fluxes.shape
    ocean_rows = field.shape[0]
    width = chunk_total * LANE
    vmem = pl.BlockSpec(memory_space=pltpu.VMEM)
    edge = pltpu.VMEM((fields + 1, rows, LANE), jnp.bfloat16)
    blocks = len(matrices)
    steps = blocks // 2
    beside = pltpu.VMEM((blocks, 2, rows, LANE), jnp.float32)
    column = pltpu.VMEM((8, LANE), jnp.float32)
    block = pltpu.VMEM((steps, 2, rows, width), jnp.float32)
    table = [tuple(int(c) for c in chunks) for chunks in chunk_table]
    return pl.pallas_call(
        lambda *refs: neighbours_kernel(steps, table, *refs),
        out_shape=[jax.ShapeDtypeStruct((fields + 1, rows, width), jnp.bfloat16)] * blocks
        + [jax.ShapeDtypeStruct((rows, width), jnp.float32)],
        in_specs=[vmem] * (5 + blocks),
        out_specs=[vmem] * (blocks + 1),
        scratch_shapes=[
            edge,
            edge,
            beside,
            beside,
            column,
            column,
            pltpu.VMEM((chunk_total, 2, ocean_rows, LANE), jnp.float32),
            pltpu.VMEM((blocks, 2, rows, width), jnp.float32),
            pltpu.VMEM((8, width), jnp.float32),
            pltpu.VMEM((blocks, 2, rows, width), jnp.float32),
            block,
            block,
            pltpu.SemaphoreType.DMA((2 * blocks + 4,)),
            pltpu.SemaphoreType.DMA((2 * blocks + 4,)),
            pltpu.SemaphoreType.DMA((6 * steps,)),
            pltpu.SemaphoreType.DMA((6 * steps,)),
        ],
        compiler_params=pltpu.CompilerParams(
            collective_id=steps - 1, has_side_effects=True, vmem_limit_bytes=VMEM_LIMIT
        ),
        name="exchange_" + str(steps),
    )(fluxes, land, field, flag_t, q, *matrices)


def neighbours_plan(
    steps, rows, fluxes, land, field, flag_t, q, first_row, row_taps, row_sums, table
):
    chunk_table, chunk_total, atmos_cols = table
    at = atmos_cols % LANE
    assert LON_REACH <= at and at + 2 * LON_REACH < LANE
    matrices = [row_matrix(first_row + d * rows, row_taps, rows) for d in range(steps, -steps - 1, -1)]
    matrices = [matrix.astype(jnp.bfloat16) for matrix in matrices]
    *pieces, surface = neighbours_call(
        fluxes,
        land,
        field,
        flag_t,
        q,
        [matrix[: field.shape[0]].T for matrix in matrices],
        chunk_table,
        chunk_total,
    )
    ocean_flux = forward_call(
        pieces, matrices, q, chunk_table, chunk_total, row_sums, flag_t
    )
    return ocean_flux, surface[:, :atmos_cols]


def exchange_plan(
    capacity, rows, fluxes, land, field, flag_t, q, first_row, row_taps, row_sums, table
):
    chunk_table, chunk_total, atmos_cols = table
    reach = LON_REACH
    wide = atmos_cols + 2 * reach
    steps = -(-capacity // rows)
    tail = capacity - rows * (steps - 1)
    count = lambda t: tail if t == steps else rows

    water_atmos = (1 - land).astype(jnp.bfloat16)
    stack = jnp.concatenate([fluxes * water_atmos[None], water_atmos[None]], axis=0)
    right = neighbour(stack[:, :, :reach], "lon", -1)
    left = neighbour(stack[:, :, atmos_cols - reach :], "lon", 1)
    filler = jnp.zeros(stack.shape[:2] + (chunk_total * LANE - wide,), stack.dtype)
    stack = jnp.concatenate([stack, right, left, filler], axis=2)

    around = {0: (0, rows)}
    pieces = {0: stack}
    for t in range(1, steps + 1):
        n = count(t)
        around[-t] = (-t * rows + rows - n, n)
        around[t] = (t * rows, n)
        pieces[-t] = shift(pieces[1 - t][:, rows - n :], "lat", 1)
        pieces[t] = shift(pieces[t - 1][:, :n], "lat", -1)
    order = sorted(around)
    matrices = {d: row_matrix(first_row - around[d][0], row_taps, around[d][1]) for d in order}

    *parts, ones = backward_call(
        field,
        flag_t,
        q,
        [matrices[d].T.astype(jnp.bfloat16) for d in order],
        chunk_table,
        chunk_total,
        wide,
    )

    def beside(start):
        edge = [part[:, :, start : start + reach] for part in parts]
        edge.append(jnp.broadcast_to(ones[None, :1, start : start + reach], (2, 1, reach)))
        return jnp.concatenate(edge, axis=1)

    from_left = neighbour(beside(atmos_cols), "lon", 1)
    from_right = neighbour(beside(atmos_cols + reach), "lon", -1)
    width = parts[0].shape[2]

    def settle(part, row, n):
        low = from_left[:, row : row + n]
        high = from_right[:, row : row + n]
        rest = ((0, 0), (0, 0))
        return (
            part
            + jnp.pad(low, rest + ((0, width - reach),))
            + jnp.pad(high, rest + ((atmos_cols - reach, width - atmos_cols),))
        )

    totals, row = {}, 0
    for d, part in zip(order, parts):
        totals[d] = settle(part, row, part.shape[1])
        row += part.shape[1]
    lon_sums = settle(jnp.broadcast_to(ones[None, :1], (2, 1, width)), row, 1)[0, 0, :atmos_cols]

    up, down = totals[steps], totals[-steps]
    for t in range(1, steps + 1):
        up, down = shift(up, "lat", 1), shift(down, "lat", -1)
        if t < steps:
            up = totals[steps - t] + jnp.pad(up, ((0, 0), (0, rows - up.shape[1]), (0, 0)))
            down = totals[t - steps] + jnp.pad(down, ((0, 0), (rows - down.shape[1], 0), (0, 0)))
    up = jnp.pad(up, ((0, 0), (0, rows - up.shape[1]), (0, 0)))
    down = jnp.pad(down, ((0, 0), (rows - down.shape[1], 0), (0, 0)))
    total = totals[0] + up + down

    ocean_flux = forward_call(
        [pieces[d] for d in order],
        [matrices[d].astype(jnp.bfloat16) for d in order],
        q,
        chunk_table,
        chunk_total,
        row_sums,
        flag_t,
    )
    lat_sums = total[1, :, wide]
    safe_surface = jnp.maximum(
        total[1, :, :atmos_cols], FLOOR_SHARE * (lat_sums[:, None] * lon_sums[None, :] + 1.0)
    )
    return ocean_flux, total[0, :, :atmos_cols] / safe_surface


def capacities_below(rows):
    return (rows, 2 * rows)


def local(
    exchange_density_arrays,
    marine_thermal_frozen_values,
    coarse_continent_flag,
    marine_continent_flag,
    parallel_source_initial,
    parallel_source_tally,
    parallel_intersect_coefs,
    meridian_source_displacement,
    meridian_source_tally,
    meridian_intersect_coefs,
):
    band_pos = lax.axis_index("lat")
    tile_pos = lax.axis_index("lon")
    bands = lax.axis_size("lat")
    atmos_rows, atmos_cols = coarse_continent_flag.shape
    ocean_rows, ocean_cols = marine_continent_flag.shape
    chunk_table, chunk_total = tile_chunks(atmos_cols, ocean_cols)

    here = lambda array, pos, count: lax.dynamic_slice_in_dim(array, pos * count, count)
    row_taps = tap_weights(
        here(parallel_source_tally, band_pos, ocean_rows),
        here(parallel_intersect_coefs, band_pos, ocean_rows),
    )
    col_taps = tap_weights(
        here(meridian_source_tally, tile_pos, ocean_cols),
        here(meridian_intersect_coefs, tile_pos, ocean_cols),
    )
    q = column_tiles(
        here(meridian_source_displacement, tile_pos, ocean_cols), col_taps, chunk_table, atmos_cols
    )
    row_sums = jnp.sum(row_taps, axis=1)[None, :]
    rows_padded = round_up(ocean_rows + 1, LANE)
    row_taps = jnp.pad(row_taps, ((0, rows_padded - ocean_rows), (0, 0)))
    first_row = here(parallel_source_initial, band_pos, ocean_rows) - band_pos * atmos_rows
    first_row = jnp.pad(first_row, (0, rows_padded - ocean_rows))

    starts = parallel_source_initial.reshape(bands, ocean_rows)
    band = jnp.arange(bands, dtype=jnp.int32)
    below = jnp.max(band * atmos_rows - starts[:, 0])
    above = jnp.max(starts[:, -1] + row_taps.shape[1] - (band + 1) * atmos_rows)
    need = jnp.maximum(below, above)
    longest = (bands - 1) * atmos_rows
    capacities = sorted({min(n, longest) for n in capacities_below(atmos_rows)} | {longest})
    choice = sum((need > n).astype(jnp.int32) for n in capacities[:-1])

    table = (chunk_table, chunk_total, atmos_cols)
    plans = [
        (lambda *operands, n=n: exchange_plan(n, atmos_rows, *operands, table)) for n in capacities
    ]
    for i, n in enumerate(capacities[:2]):
        if n == (i + 1) * atmos_rows:
            plans[i] = lambda *operands, i=i: neighbours_plan(i + 1, atmos_rows, *operands, table)
    ocean_flux, surface = lax.switch(
        choice,
        plans,
        exchange_density_arrays,
        coarse_continent_flag,
        with_layout_constraint(marine_thermal_frozen_values[0], Layout((0, 1))),
        marine_continent_flag.T,
        q,
        first_row,
        row_taps,
        row_sums,
    )
    return ocean_flux.transpose(0, 2, 1), surface[None]


def solution(mesh):
    fields = P(("group", "fld"), "lat", "lon")
    cells = P("lat", "lon")
    return jax.shard_map(
        local,
        mesh=mesh,
        in_specs=(fields, fields, cells, cells) + (P(),) * 6,
        out_specs=(fields, fields),
        check_vma=False,
    )
```
